256 devices in a mesh: task: 8 (over y, x_hi), blk: 16 (over z, core), comp: 2 (over x_lo).
Axes of the slice: x: 4 (x_hi: 2, x_lo: 2; x = x_hi * 2 + x_lo), y: 4, z: 8, core: 2. Of those that a mesh axis runs over, the one named last changes fastest.
Arguments:
- query_component_embeddings: bfloat16 [32768, 512], P(('task', 'blk'), 'comp'), parts along dimension 0, may hold values from -13 to 13
- candidate_component_embeddings: bfloat16 [32768, 512], P(('task', 'blk'), 'comp'), parts along dimension 0, may hold values from -1.5 to 1.5
- query_routing_features: bfloat16 [8, 32768], P('comp', ('task', 'blk')), parts along dimension 1, may hold values from -1.5 to 1.5
- candidate_routing_features: bfloat16 [8, 32768], P('comp', ('task', 'blk')), parts along dimension 1, may hold values from -1.5 to 1.5
- own_logit_coefficient: float32 [8], replicated, may hold values from 0.5 to 2.5
- loss_divisor_scale: float32 [8], P('task'), parts along dimension 0, may hold values from 0.1 to 0.2
- target_candidate_index: int32 [32768], P(('task', 'blk')), parts along dimension 0, may hold values from 0 to 4095, each once
Outputs:
- losses: float32 [32768], P(('task', 'blk')), parts along dimension 0
- user_grad: float32 [32768, 512], P(('task', 'blk'), 'comp'), parts along dimension 0
- item_grad: float32 [32768, 512], P(('task', 'blk'), 'comp'), parts along dimension 0
- user_gate_grad: float32 [8, 32768], P('comp', ('task', 'blk')), parts along dimension 1
- item_gate_grad: float32 [8, 32768], P('comp', ('task', 'blk')), parts along dimension 1
The draws below stay inside these ranges and needn't reach their ends.
There are 8 independent parts, one for each index of `task`. The reference program is written for one: setup_inputs(seed, part) draws one part's arguments, and reference() takes and returns one part's arrays. A program takes and returns all parts, laid end to end along the dimension named above; an argument that names none is the same for every part. Nothing has to cross between parts.
Inputs may be any that keep to these rules, and one draw needn't show every extreme that they name: `target_candidate_index`: each item is the positive of exactly one user.
All inputs are finite; a program needn't handle non-finite values.
Results may differ from the reference program's by a relative error of at most 0.0029.
Values may be sent and summed in bfloat16 or wider, within the bound.
A program may use at most 64 MiB of HBM per device.

```python
import math
import jax
import jax.numpy as jnp
from jax import lax

K = 8
E = 64
U_DEV = 256
USERS = 4096
ITEMS = 4096
N_BLK = 16


def shared_items(key):
    base_items = jax.random.normal(key, (ITEMS, K * E), jnp.float32) * E ** (-0.25)
    return jnp.clip(base_items, -1.4, 1.4)


def draw_candidate_component_embeddings(key, part):
    base_items = shared_items(key)
    return base_items.astype(jnp.bfloat16)


def draw_query_component_embeddings(key, part):
    key = jax.random.fold_in(key, 7)
    user_draw = jnp.clip(jax.random.normal(key, (USERS, K * E), jnp.float32) * E ** (-0.25), -1.4, 1.4) * 0.2
    return user_draw.astype(jnp.bfloat16)


def steps_of(own_key, extent, cuts, smallest, high):
    def one(position, blocks):
        draws = jax.random.uniform(jax.random.fold_in(jax.random.fold_in(own_key, 6), position), (blocks,), jnp.float32, smallest / len(cuts), high / len(cuts))
        return jnp.repeat(jnp.exp(draws), extent[position] // blocks).reshape((-1,) + (1,) * (len(extent) - position - 1))

    factor_of = one(*cuts[0])
    for cut in cuts[1:]:
        factor_of = factor_of * one(*cut)
    return factor_of


def setup_inputs(seed: int = 0, part: int = 0) -> dict:
    keys = jax.random.split(jax.random.key(seed), 8)
    part_splits = jax.random.split(jax.random.fold_in(keys[7], part), 8)
    query_component_embeddings = draw_query_component_embeddings(jax.random.fold_in(jax.random.fold_in(keys[7], part), 71), part)
    candidate_component_embeddings = draw_candidate_component_embeddings(jax.random.fold_in(jax.random.fold_in(keys[7], part), 71), part)
    query_routing_features = jnp.clip(jax.random.uniform(part_splits[2], (K, USERS), jnp.float32, -1.5, 1.5) * steps_of(part_splits[2], (K, USERS), ((0, 2), (1, 16)), -0.4, 0.0), -1.5, 1.5).astype(jnp.bfloat16)
    candidate_routing_features = jnp.clip(jax.random.uniform(part_splits[3], (K, ITEMS), jnp.float32, -1.5, 1.5) * steps_of(part_splits[3], (K, ITEMS), ((0, 2), (1, 16)), -0.4, 0.0), -1.5, 1.5).astype(jnp.bfloat16)
    own_logit_coefficient = jnp.clip(jax.random.uniform(keys[4], (K,), jnp.float32, 0.5, 2.5), 0.5, 2.5)
    loss_divisor_scale = jnp.clip(jnp.exp(jax.random.uniform(part_splits[5], (1,), jnp.float32, math.log(0.1), math.log(0.2))), 0.1, 0.2)
    target_candidate_index = jax.random.permutation(part_splits[6], ITEMS).astype(jnp.int32)
    return dict(query_component_embeddings=query_component_embeddings, candidate_component_embeddings=candidate_component_embeddings, query_routing_features=query_routing_features, candidate_routing_features=candidate_routing_features, own_logit_coefficient=own_logit_coefficient, loss_divisor_scale=loss_divisor_scale, target_candidate_index=target_candidate_index)


def reference(query_component_embeddings, candidate_component_embeddings, query_routing_features, candidate_routing_features, own_logit_coefficient, loss_divisor_scale, target_candidate_index):
    mixture_count = query_routing_features.shape[0]
    comp_width = query_component_embeddings.shape[1] // mixture_count
    item_count = candidate_component_embeddings.shape[0]
    user_count = query_component_embeddings.shape[0]
    normalizer_scale = loss_divisor_scale[0]
    item_split = candidate_component_embeddings.astype(jnp.float32).reshape(item_count, mixture_count, comp_width)
    gate_items = candidate_routing_features.astype(jnp.float32)
    item_ids = jnp.arange(item_count, dtype=jnp.int32)
    slope = own_logit_coefficient[:, None, None]

    def one_block(running, pieces):
        user_block, gate_block, pos_block = pieces
        user_split = user_block.astype(jnp.float32).reshape(-1, mixture_count, comp_width)
        logits = jnp.einsum("rke,ike->kri", user_split, item_split)
        bent_logit = jnp.tanh(logits)
        weight_matrix = jnp.exp(gate_block.astype(jnp.float32)[:, :, None] + gate_items[:, None, :] + slope * bent_logit)
        denominator = jnp.sum(weight_matrix, axis=0)
        pair_score = jnp.sum(weight_matrix * logits, axis=0) / denominator
        scaled = pair_score / normalizer_scale
        row_top = jnp.max(scaled, axis=1, keepdims=True)
        log_total = row_top[:, 0] + jnp.log(jnp.sum(jnp.exp(scaled - row_top), axis=1))
        is_positive = (pos_block[:, None] == item_ids[None, :]).astype(jnp.float32)
        user_loss = log_total - jnp.sum(is_positive * pair_score, axis=1) / normalizer_scale
        softmax_grad = (jnp.exp(scaled - log_total[:, None]) - is_positive) / normalizer_scale
        gate_share = weight_matrix / denominator[None]
        logit_gap = logits - pair_score[None]
        gate_grad = softmax_grad[None] * gate_share * logit_gap
        raw_grad = softmax_grad[None] * gate_share * (1.0 + logit_gap * slope * (1.0 - bent_logit * bent_logit))
        logit_grad = lax.optimization_barrier(raw_grad.astype(jnp.bfloat16)).astype(jnp.float32)
        user_part = jnp.einsum("kri,ike->rke", logit_grad, item_split)
        item_part = jnp.einsum("kri,rke->ike", logit_grad, user_split)
        item_acc, gate_acc = running
        item_acc = item_acc + item_part.reshape(item_count, mixture_count * comp_width)
        gate_acc = gate_acc + jnp.sum(gate_grad, axis=1)
        return (item_acc, gate_acc), (user_loss, user_part.reshape(user_part.shape[0], mixture_count * comp_width), jnp.sum(gate_grad, axis=2))

    user_blocks = query_component_embeddings.reshape(N_BLK, U_DEV, mixture_count * comp_width)
    gate_blocks = query_routing_features.reshape(mixture_count, N_BLK, U_DEV).transpose(1, 0, 2)
    pos_blocks = target_candidate_index.reshape(N_BLK, U_DEV)
    start = (jnp.zeros((item_count, mixture_count * comp_width), jnp.float32), jnp.zeros((mixture_count, item_count), jnp.float32))
    (item_grad, item_gate_grad), (losses, user_grad, user_gate_parts) = lax.scan(one_block, start, (user_blocks, gate_blocks, pos_blocks))
    user_gate_grad = user_gate_parts.transpose(1, 0, 2).reshape(mixture_count, user_count)
    return losses.reshape(user_count), user_grad.reshape(user_count, mixture_count * comp_width), item_grad, user_gate_grad, item_gate_grad
```

```python
import jax
import jax.numpy as jnp
from jax import lax
from jax.experimental import pallas as pl
from jax.experimental.pallas import tpu as pltpu
from jax.sharding import PartitionSpec as P

MESH = pl.DeviceIdType.MESH
LOG2E = 1.4426950408889634
F32, BF16 = jnp.float32, jnp.bfloat16
NZ = 8
UB = 256
US = 512
CH = 128
K = 8
ROWS = 16
NT = (((1,), (1,)), ((), ()))


def kernel(
    q_ref, c_ref, gq_ref, gc_ref, slope_ref, t_ref, tgt_ref,
    loss_ref, ug_ref, ig_ref, ugate_ref, igate_ref,
    qall, ugall, call, giall, gstage, gpad, git, qm, gub, tgtb,
    logit, weight, score, dinv, mx, ps, stat, ltb,
    lg, igp, ugv, uacc, ibuf, sbuf, rbuf, igsend, igrecv,
    urecv, ured, usend, uxrecv, ifin, irecv, igx, ugsend, ugrecv,
    x_s, x_r, q_s, q_r, u_s, u_r, gi_s, gi_r, ag_s, ag_r, st_s, st_r,
    rs_s, rs_r, ig_s, ig_r, fx_s, fx_r, ugs_s, ugs_r,
):
    blk = lax.axis_index("blk")
    x = lax.axis_index("comp")
    z = blk // 2
    c = lax.rem(blk, 2)
    me = 2 * x + c

    def dev(zz, cc, xx):
        return {"blk": lax.rem(zz + NZ, NZ) * 2 + cc, "comp": xx}

    def rc(src, dst, ss, rs, device):
        return pltpu.make_async_remote_copy(
            src_ref=src, dst_ref=dst, send_sem=ss, recv_sem=rs, device_id=device, device_id_type=MESH
        )

    xp, cp, dp = dev(z, c, 1 - x), dev(z, 1 - c, x), dev(z, 1 - c, 1 - x)
    quad = (xp, cp, dp)

    own_rows = pl.ds(pl.multiple_of(x * CH, CH), CH)
    peer_rows = pl.ds(pl.multiple_of((1 - x) * CH, CH), CH)
    call[z, x] = c_ref[own_rows, :]
    qall[c, x] = q_ref[...]
    gc = gc_ref[...].astype(F32)
    gc = jnp.concatenate([gc, gc], axis=0)
    low = jnp.broadcast_to(x, (8, CH)) == 0
    giall[z, x] = jnp.where(low, gc[:, :CH], gc[:, CH:])
    gstage[...] = jnp.where(low, gc[:, CH:], gc[:, :CH])
    gq = gq_ref[...].astype(F32)
    ugall[me] = jnp.concatenate([gq, jnp.broadcast_to(tgt_ref[...].astype(F32), (4, UB))], axis=0)

    barrier = pltpu.get_barrier_semaphore()
    for d in range(1, NZ):
        pl.semaphore_signal(barrier, inc=1, device_id=dev(z + d, c, x), device_id_type=MESH)
    for peer in quad:
        pl.semaphore_signal(barrier, inc=1, device_id=peer, device_id_type=MESH)
    pl.semaphore_wait(barrier, NZ - 1 + 3)

    def hop(dr, s, h):
        step = 1 - 2 * dr
        o = lax.rem(z - step * (s - 1) + NZ, NZ)
        return rc(
            call.at[o, h], call.at[o, h], ag_s.at[dr, s - 1, h], ag_r.at[dr, s - 1, h],
            dev(z + step, c, x),
        )

    x_item = rc(c_ref.at[peer_rows, :], call.at[z, x], x_s.at[0], x_r.at[0], xp)
    x_gate = rc(gstage, giall.at[z, x], x_s.at[1], x_r.at[1], xp)
    q_x = rc(q_ref, qall.at[c, x], q_s.at[0], q_r.at[0], xp)
    q_c = rc(q_ref, qall.at[c, x], q_s.at[1], q_r.at[1], cp)
    q_f = rc(qall.at[c, 1 - x], qall.at[c, 1 - x], q_s.at[2], q_r.at[2], cp)
    u_sends = [rc(ugall.at[me], ugall.at[me], u_s.at[i], u_r.at[i], quad[i]) for i in range(3)]
    x_item.start()
    x_gate.start()
    hop(0, 1, x).start()
    hop(1, 1, x).start()
    q_x.start()
    q_c.start()
    for s in u_sends:
        s.start()

    def gi_copy(d):
        return rc(giall.at[z], giall.at[z], gi_s.at[d], gi_r.at[d], dev(z + d, c, x))

    x_item.wait_recv()
    hop(0, 1, 1 - x).start()
    hop(1, 1, 1 - x).start()
    x_gate.wait_recv()

    def gi_start(d, carry):
        gi_copy(d).start()
        return carry

    lax.fori_loop(1, NZ, gi_start, 0)
    q_x.wait_recv()
    q_f.start()
    for s in u_sends:
        s.wait_recv()

    gpad[...] = jnp.zeros_like(gpad)
    mx[...] = jnp.full(mx.shape, -jnp.inf, F32)
    ps[...] = jnp.zeros_like(ps)
    uacc[...] = jnp.zeros_like(uacc)
    ugv[...] = jnp.zeros_like(ugv)
    for k in range(K):
        h, r = k // 4, k % 4
        row = jnp.concatenate([ugall[2 * h, r : r + 1, :], ugall[2 * h + 1, r : r + 1, :]], axis=1)
        gub[k] = jnp.broadcast_to(row * LOG2E, (8, US))
    tgtb[...] = jnp.broadcast_to(
        jnp.concatenate([ugall[0, 4:5, :], ugall[1, 4:5, :]], axis=1), (8, US)
    )
    q_c.wait_recv()
    q_f.wait_recv()
    lane = lax.broadcasted_iota(jnp.int32, (UB, CH), 1)
    for h in range(2):
        for p in range(2):
            for cc in range(2):
                pair = qall[cc, h, :, p * CH : (p + 1) * CH].astype(F32)
                k = 4 * h + 2 * p
                qm[k, cc * UB : (cc + 1) * UB, :] = jnp.where(lane < 64, pair, 0.0).astype(BF16)
                qm[k + 1, cc * UB : (cc + 1) * UB, :] = jnp.where(lane < 64, 0.0, pair).astype(BF16)

    inv_t = 1.0 / jnp.full((8, US), t_ref[0], F32)
    inv_t16 = jnp.concatenate([inv_t, inv_t], axis=0)
    row_iota = lax.broadcasted_iota(jnp.int32, (ROWS, US), 0)

    def twice(v):
        return jnp.concatenate([v, v], axis=0)

    def is_positive(o, r):
        ids = row_iota + ((o * 2 + c) * UB + x * CH + r * ROWS)
        return twice(tgtb[...]) == ids.astype(F32)

    def forward(j, carry):
        s = (j + 1) // 2
        odd = lax.rem(j, 2) == 1

        @pl.when(odd)
        def _():
            for dr in range(2):
                for h in range(2):
                    last = 4 if h == dr else 3

                    @pl.when(s <= last)
                    def _():
                        hop(dr, s, h).wait_recv()

                    @pl.when(s < last)
                    def _():
                        hop(dr, s + 1, h).start()

            gi_copy(s).wait_recv()

            @pl.when(s < 4)
            def _():
                gi_copy(NZ - s).wait_recv()

        o = lax.rem(z + NZ + jnp.where(odd, -s, s), NZ)
        gpad[0:8, :] = giall[o, 0]
        gpad[8:16, :] = giall[o, 1]
        git[...] = gpad[...].T * LOG2E
        for k in range(K):
            h, p = k // 4, (k % 4) // 2
            logit[o, k] = lax.dot_general(
                call[o, h, :, p * CH : (p + 1) * CH], qm[k], NT, preferred_element_type=F32
            )

        def rows_of(r, carry):
            top, pos = carry
            rows = pl.ds(pl.multiple_of(r * ROWS, ROWS), ROWS)
            den = num = None
            gcols = git[rows, :]
            for k in range(K):
                col = (k // 4) * 8 + k % 4
                l = logit[o, k, rows, :]
                e = jnp.tanh(l) * (slope_ref[k] * LOG2E) + gcols[:, col : col + 1] + twice(gub[k])
                w = jnp.exp2(e)
                weight[o, k, rows, :] = w
                wl = w * l
                den = w if den is None else den + w
                num = wl if num is None else num + wl
            di = 1.0 / den
            sc = num * di
            dinv[o, rows, :] = di
            score[o, rows, :] = sc
            hit = jnp.where(is_positive(o, r), sc, 0.0)
            return (
                jnp.maximum(top, jnp.maximum(sc[:8], sc[8:])),
                pos + hit[:8] + hit[8:],
            )

        top, pos = lax.fori_loop(0, CH // ROWS, rows_of, (mx[...], ps[...]))
        mx[...] = top
        ps[...] = pos
        return carry

    lax.fori_loop(0, NZ, forward, 0)

    top = jnp.max(mx[...], axis=0, keepdims=True)
    scale2 = inv_t * LOG2E
    shift = jnp.broadcast_to(top, (8, US)) * scale2

    def sum_exp(i, acc):
        o = i // 4
        rows = pl.ds(pl.multiple_of(lax.rem(i, 4) * 32, 32), 32)
        v = score[o, rows, :]
        for m in range(4):
            acc = acc + jnp.exp2(v[m * 8 : (m + 1) * 8] * scale2 - shift)
        return acc

    total = lax.fori_loop(0, NZ * 4, sum_exp, jnp.zeros((8, US), F32))
    stat[me, 0:1, :] = top
    stat[me, 1:2, :] = jnp.sum(total, axis=0, keepdims=True)
    stat[me, 2:3, :] = jnp.sum(ps[...], axis=0, keepdims=True)
    stat[me, 3:8, :] = jnp.zeros((5, US), F32)
    st_sends = [rc(stat.at[me], stat.at[me], st_s.at[i], st_r.at[i], quad[i]) for i in range(3)]
    for s in st_sends:
        s.start()
    for s in st_sends:
        s.wait_recv()
    st = [stat[i] for i in range(4)]
    all_top = jnp.maximum(jnp.maximum(st[0][0:1], st[1][0:1]), jnp.maximum(st[2][0:1], st[3][0:1]))
    inv_row = inv_t[0:1]
    all_sum = all_pos = None
    for i in range(4):
        part = st[i][1:2] * jnp.exp((st[i][0:1] - all_top) * inv_row)
        all_sum = part if all_sum is None else all_sum + part
        all_pos = st[i][2:3] if all_pos is None else all_pos + st[i][2:3]
    log_total = all_top * inv_row + jnp.log(all_sum)
    loss = log_total - all_pos * inv_row
    loss_ref[...] = jnp.where(jnp.broadcast_to(c, (1, UB)) == 0, loss[:, :UB], loss[:, UB:])
    ltb[...] = jnp.broadcast_to(log_total * LOG2E, (8, US))

    ones_row = lax.broadcasted_iota(jnp.int32, (K, K * CH), 0)
    ones_col = lax.broadcasted_iota(jnp.int32, (K, K * CH), 1) // CH
    ones = jnp.where(ones_row == ones_col, 1.0, 0.0).astype(BF16)

    def ig_copy(d):
        return rc(igsend.at[d], igrecv.at[d], ig_s.at[d], ig_r.at[d], dev(z + d, c, x))

    def rs_copy(dr, i, h):
        return rc(
            sbuf.at[dr, i, h], rbuf.at[dr, i, h], rs_s.at[dr, i, h], rs_r.at[dr, i, h],
            dev(z + 2 * dr - 1, c, x),
        )

    def backward(j, carry):
        d = 4 - (j + 1) // 2
        odd = lax.rem(j, 2) == 1
        o = lax.rem(z + NZ + jnp.where(odd, -d, d), NZ)

        def rows_of(r, carry):
            rows = pl.ds(pl.multiple_of(r * ROWS, ROWS), ROWS)
            sc = score[o, rows, :]
            soft = jnp.exp2(sc * twice(scale2) - twice(ltb[...]))
            soft = jnp.where(is_positive(o, r), soft - 1.0, soft) * inv_t16
            share = soft * dinv[o, rows, :]
            for k in range(K):
                l = logit[o, k, rows, :]
                t = jnp.tanh(l)
                g = weight[o, k, rows, :] * share
                gg = g * (l - sc)
                sk = slope_ref[k]
                out = g + gg * (sk - (t * t) * sk)
                lg[k, rows, :] = out.astype(BF16)
                ugv[k] = ugv[k] + (gg[:8] + gg[8:])
                igp[rows, k * CH : (k + 1) * CH] = (gg[:, 0:128] + gg[:, 128:256]) + (
                    gg[:, 256:384] + gg[:, 384:512]
                )
            return carry

        lax.fori_loop(0, CH // ROWS, rows_of, 0)
        for h in range(2):
            for p in range(2):
                k = 4 * h + 2 * p
                ibuf[h, :, p * CH : (p + 1) * CH] = jnp.dot(
                    lg[k], qm[k], preferred_element_type=F32
                ) + jnp.dot(lg[k + 1], qm[k + 1], preferred_element_type=F32)
        hi = igp[...].astype(BF16)
        lo = (igp[...] - hi.astype(F32)).astype(BF16)
        gate = lax.dot_general(ones, hi, NT, preferred_element_type=F32) + lax.dot_general(
            ones, lo, NT, preferred_element_type=F32
        )

        to = lax.rem(o - z + NZ, NZ)

        @pl.when(j < 7)
        def _():
            igsend[to] = gate
            ig_copy(to).start()

        @pl.when(j == 7)
        def _():
            igrecv[0] = gate

        @pl.when(j == 0)
        def _():
            for h in range(2):
                sbuf[h, 3, h] = ibuf[h].astype(BF16)
                rs_copy(h, 3, h).start()

        @pl.when((j > 0) & (j < 7))
        def _():
            dr = 1 - lax.rem(j, 2)
            for h in range(2):

                @pl.when((d < 3) | (dr == h))
                def _():
                    rs_copy(dr, d, h).wait_recv()
                    ibuf[h] = ibuf[h] + rbuf[dr, d, h].astype(F32)

                sbuf[dr, d - 1, h] = ibuf[h].astype(BF16)
                rs_copy(dr, d - 1, h).start()

        for h in range(2):
            for p in range(2):
                k = 4 * h + 2 * p
                ct = call[o, h, :, p * CH : (p + 1) * CH].T
                for kk in range(2):
                    part = jnp.dot(
                        ct[kk * 64 : (kk + 1) * 64], lg[k + kk], preferred_element_type=F32
                    )
                    at = slice((k + kk) * 64, (k + kk + 1) * 64)
                    uacc[0, at, :] += part[:, :UB]
                    uacc[1, at, :] += part[:, UB:]
        return carry

    lax.fori_loop(0, NZ, backward, 0)

    u_core = rc(uacc.at[1 - c], urecv, fx_s.at[0], fx_r.at[0], cp)
    u_core.start()
    for k in range(K):
        ugsend[k : k + 1, :] = jnp.sum(ugv[k], axis=0, keepdims=True)
    ug_sends = [rc(ugsend, ugrecv.at[i], ugs_s.at[i], ugs_r.at[i], quad[i]) for i in range(3)]
    for s in ug_sends:
        s.start()
    u_core.wait_recv()
    ured[...] = uacc[c] + urecv[...]
    half_other = pl.ds(pl.multiple_of((1 - x) * UB, UB), UB)
    half_own = pl.ds(pl.multiple_of(x * UB, UB), UB)
    usend[...] = ured[half_other, :].astype(BF16)
    u_x = rc(usend, uxrecv, fx_s.at[1], fx_r.at[1], xp)
    u_x.start()

    for dr in range(2):
        for h in range(2):
            rs_copy(dr, 0, h).wait_recv()
    for h in range(2):
        ifin[h] = ibuf[h] + (rbuf[0, 0, h].astype(F32) + rbuf[1, 0, h].astype(F32))
    i_x = rc(ifin.at[1 - x], irecv, fx_s.at[2], fx_r.at[2], xp)
    i_x.start()
    for d in range(1, NZ):
        ig_copy(d).wait_recv()
    gate = igrecv[0]
    for d in range(1, NZ):
        gate = gate + igrecv[d]
    igx[0] = gate
    ig_x = rc(igx.at[0], igx.at[1], fx_s.at[3], fx_r.at[3], xp)
    ig_x.start()
    ig_ref[own_rows, :] = ifin[x]

    for s in ug_sends:
        s.wait_recv()
    ugate = (ugsend[...] + ugrecv[0]) + (ugrecv[1] + ugrecv[2])
    ugate = jnp.where(jnp.broadcast_to(c, (K, UB)) == 0, ugate[:, :UB], ugate[:, UB:])
    ugate_ref[...] = jnp.where(jnp.broadcast_to(x, (4, UB)) == 0, ugate[:4], ugate[4:])

    ig_x.wait_recv()
    mine, theirs = igx[0], igx[1]
    upper = jnp.concatenate([mine, theirs], axis=1)[:4]
    lower = jnp.concatenate([theirs, mine], axis=1)[4:]
    igate_ref[...] = jnp.where(jnp.broadcast_to(x, (4, UB)) == 0, upper, lower)

    u_x.wait_recv()
    ug_ref[...] = (ured[half_own, :] + uxrecv[...].astype(F32)).T
    i_x.wait_recv()
    ig_ref[peer_rows, :] = irecv[...]

    for s in (x_item, x_gate, q_x, q_c, q_f, *u_sends, *st_sends, u_core, u_x, i_x, ig_x, *ug_sends):
        s.wait_send()
    for d in range(1, NZ):
        gi_copy(d).wait_send()
        ig_copy(d).wait_send()
    for dr in range(2):
        for h in range(2):
            for s in range(1, 5 if h == dr else 4):
                hop(dr, s, h).wait_send()
                rs_copy(dr, s - 1, h).wait_send()


def body(query, candidate, query_gate, candidate_gate, slope, scale, target):
    vmem = pl.BlockSpec(memory_space=pltpu.VMEM)
    smem = pl.BlockSpec(memory_space=pltpu.SMEM)
    dma = pltpu.SemaphoreType.DMA
    scratch = [
        pltpu.VMEM((2, 2, UB, UB), BF16),
        pltpu.VMEM((4, 8, UB), F32),
        pltpu.VMEM((NZ, 2, CH, UB), BF16),
        pltpu.VMEM((NZ, 2, 8, CH), F32),
        pltpu.VMEM((8, CH), F32),
        pltpu.VMEM((CH, CH), F32),
        pltpu.VMEM((CH, CH), F32),
        pltpu.VMEM((K, US, CH), BF16),
        pltpu.VMEM((K, 8, US), F32),
        pltpu.VMEM((8, US), F32),
        pltpu.VMEM((NZ, K, CH, US), F32),
        pltpu.VMEM((NZ, K, CH, US), F32),
        pltpu.VMEM((NZ, CH, US), F32),
        pltpu.VMEM((NZ, CH, US), F32),
        pltpu.VMEM((8, US), F32),
        pltpu.VMEM((8, US), F32),
        pltpu.VMEM((4, 8, US), F32),
        pltpu.VMEM((8, US), F32),
        pltpu.VMEM((K, CH, US), BF16),
        pltpu.VMEM((CH, K * CH), F32),
        pltpu.VMEM((K, 8, US), F32),
        pltpu.VMEM((2, US, UB), F32),
        pltpu.VMEM((2, CH, UB), F32),
        pltpu.VMEM((2, 4, 2, CH, UB), BF16),
        pltpu.VMEM((2, 4, 2, CH, UB), BF16),
        pltpu.VMEM((NZ, K, CH), F32),
        pltpu.VMEM((NZ, K, CH), F32),
        pltpu.VMEM((US, UB), F32),
        pltpu.VMEM((US, UB), F32),
        pltpu.VMEM((UB, UB), BF16),
        pltpu.VMEM((UB, UB), BF16),
        pltpu.VMEM((2, CH, UB), F32),
        pltpu.VMEM((CH, UB), F32),
        pltpu.VMEM((2, K, CH), F32),
        pltpu.VMEM((K, US), F32),
        pltpu.VMEM((3, K, US), F32),
        dma((2,)), dma((2,)),
        dma((3,)), dma((3,)),
        dma((3,)), dma((3,)),
        dma((NZ,)), dma((NZ,)),
        dma((2, 4, 2)), dma((2, 4, 2)),
        dma((3,)), dma((3,)),
        dma((2, 4, 2)), dma((2, 4, 2)),
        dma((NZ,)), dma((NZ,)),
        dma((4,)), dma((4,)),
        dma((3,)), dma((3,)),
    ]
    loss, ug, ig, ugate, igate = pl.pallas_call(
        kernel,
        out_shape=(
            jax.ShapeDtypeStruct((1, UB), F32),
            jax.ShapeDtypeStruct((UB, UB), F32),
            jax.ShapeDtypeStruct((UB, UB), F32),
            jax.ShapeDtypeStruct((4, UB), F32),
            jax.ShapeDtypeStruct((4, UB), F32),
        ),
        in_specs=[vmem, vmem, vmem, vmem, smem, smem, vmem],
        out_specs=(vmem,) * 5,
        scratch_shapes=scratch,
        compiler_params=pltpu.CompilerParams(
            collective_id=0, has_side_effects=True, vmem_limit_bytes=60 * 1024 * 1024
        ),
    )(query, candidate, query_gate, candidate_gate, slope, scale, target.reshape(1, UB))
    return loss.reshape(UB), ug, ig, ugate, igate


def solution(mesh):
    in_specs = (
        P(("task", "blk"), "comp"),
        P(("task", "blk"), "comp"),
        P("comp", ("task", "blk")),
        P("comp", ("task", "blk")),
        P(),
        P("task"),
        P(("task", "blk")),
    )
    out_specs = (
        P(("task", "blk")),
        P(("task", "blk"), "comp"),
        P(("task", "blk"), "comp"),
        P("comp", ("task", "blk")),
        P("comp", ("task", "blk")),
    )
    return jax.shard_map(body, mesh=mesh, in_specs=in_specs, out_specs=out_specs, check_vma=False)
```

```python
import jax
import jax.numpy as jnp
from jax import lax
from jax.experimental import pallas as pl
from jax.experimental.pallas import tpu as pltpu
from jax.sharding import PartitionSpec as P

MESH = pl.DeviceIdType.MESH
LOG2E = 1.4426950408889634
F32, BF16 = jnp.float32, jnp.bfloat16
NZ = 8
UB = 256
US = 512
CH = 128
SLOT = CH + 16
PIECES = ((0, 80), (80, 64))
K = 8
ROWS = 16
NT = (((1,), (1,)), ((), ()))


def kernel(
    q_ref, c_ref, gq_ref, gc_ref, slope_ref, t_ref, tgt_ref,
    loss_ref, ug_ref, ig_ref, ugate_ref, igate_ref,
    qall, ugall, call, xstage, gpad, git, ctall, qm, gub, tgtb,
    logit, weight, score, dinv, mx, sm, ps, stat, ltb,
    lg, igp, ugv, uacc, ibk, sbuf, rbuf, gsend, grecv,
    urecv, ukeep, usend, uxrecv, isend, irecv, igx, ugsend, ugrecv,
    x_s, x_r, q_s, q_r, u_s, u_r, ag_s, ag_r, st_s, st_r,
    rs_s, rs_r, g_s, g_r, uc_s, uc_r, ux_s, ux_r, fx_s, fx_r, ugs_s, ugs_r,
):
    blk = lax.axis_index("blk")
    x = lax.axis_index("comp")
    z = blk // 2
    c = lax.rem(blk, 2)
    me = 2 * x + c

    def dev(zz, cc, xx):
        return {"blk": lax.rem(zz + NZ, NZ) * 2 + cc, "comp": xx}

    def rc(src, dst, ss, rs, device):
        return pltpu.make_async_remote_copy(
            src_ref=src, dst_ref=dst, send_sem=ss, recv_sem=rs, device_id=device, device_id_type=MESH
        )

    xp, cp, dp = dev(z, c, 1 - x), dev(z, 1 - c, x), dev(z, 1 - c, 1 - x)
    quad = (xp, cp, dp)

    barrier = pltpu.get_barrier_semaphore()
    near = [dev(z + d, c, x) for d in (-2, -1, 1, 2)] + [dev(z + d, c, 1 - x) for d in (-1, 1)]
    for peer in (*quad, *near):
        pl.semaphore_signal(barrier, inc=1, device_id=peer, device_id_type=MESH)

    own_rows = pl.ds(pl.multiple_of(x * CH, CH), CH)
    peer_rows = pl.ds(pl.multiple_of((1 - x) * CH, CH), CH)
    gc = gc_ref[...].astype(F32)
    gc = jnp.concatenate([gc, gc], axis=0)
    gc = jnp.concatenate([gc, gc], axis=0)
    low = jnp.broadcast_to(x, (16, CH)) == 0
    blank = jnp.zeros((16, CH), F32)
    own_gate = jnp.concatenate([jnp.where(low, gc[:, :CH], gc[:, CH:]), blank], axis=1)
    peer_gate = jnp.concatenate([jnp.where(low, gc[:, CH:], gc[:, :CH]), blank], axis=1)
    call[z, x, :CH, :] = c_ref[own_rows, :]
    call[z, x, CH:, :] = own_gate.astype(BF16)
    xstage[:CH, :] = c_ref[peer_rows, :]
    xstage[CH:, :] = peer_gate.astype(BF16)
    qall[c, x] = q_ref[...]
    gq = gq_ref[...].astype(F32)
    ugall[me] = jnp.concatenate([gq, jnp.broadcast_to(tgt_ref[...].astype(F32), (4, UB))], axis=0)

    pl.semaphore_wait(barrier, len(quad) + len(near))

    def hop(dr, s, hh, n):
        step = 1 - 2 * dr
        o = lax.rem(z - step * (s - 1) + NZ, NZ)
        h = x if hh == 0 else 1 - x
        at = call.at[o, h, pl.ds(*PIECES[n]), :]
        return rc(at, at, ag_s.at[dr, s - 1, hh, n], ag_r.at[dr, s - 1, hh, n], dev(z + step, c, x))

    x_item = rc(xstage, call.at[z, x], x_s.at[0], x_r.at[0], xp)
    q_x = rc(q_ref, qall.at[c, x], q_s.at[0], q_r.at[0], xp)
    q_c = rc(q_ref, qall.at[c, x], q_s.at[1], q_r.at[1], cp)
    q_f = rc(qall.at[c, 1 - x], qall.at[c, 1 - x], q_s.at[2], q_r.at[2], cp)
    u_sends = [rc(ugall.at[me], ugall.at[me], u_s.at[i], u_r.at[i], quad[i]) for i in range(3)]
    x_item.start()
    for n in range(2):
        hop(0, 1, 0, n).start()
        hop(1, 1, 0, n).start()
    q_x.start()
    for s in u_sends:
        s.start()
    q_c.start()

    gpad[...] = jnp.zeros_like(gpad)
    mx[...] = jnp.full(mx.shape, -3.0e38, F32)
    sm[...] = jnp.zeros_like(sm)
    ps[...] = jnp.zeros_like(ps)
    uacc[...] = jnp.zeros_like(uacc)
    ugv[...] = jnp.zeros_like(ugv)
    lg[1] = jnp.zeros((K, CH, US), BF16)

    x_item.wait_recv()
    for n in range(2):
        hop(0, 1, 1, n).start()
        hop(1, 1, 1, n).start()
    q_x.wait_recv()
    q_f.start()

    lane = lax.broadcasted_iota(jnp.int32, (UB, CH), 1)

    def mask_users(cc, h):
        for p in range(2):
            pair = qall[cc, h, :, p * CH : (p + 1) * CH].astype(F32)
            k = 4 * h + 2 * p
            rows = pl.ds(pl.multiple_of(cc * UB, UB), UB)
            qm[k, rows, :] = jnp.where(lane < 64, pair, 0.0).astype(BF16)
            qm[k + 1, rows, :] = jnp.where(lane < 64, 0.0, pair).astype(BF16)

    for h in range(2):
        mask_users(c, h)
    for s in u_sends:
        s.wait_recv()
    for k in range(K):
        h, r = k // 4, k % 4
        row = jnp.concatenate([ugall[2 * h, r : r + 1, :], ugall[2 * h + 1, r : r + 1, :]], axis=1)
        gub[k] = jnp.broadcast_to(row * LOG2E, (8, US))
    tgtb[...] = jnp.broadcast_to(
        jnp.concatenate([ugall[0, 4:5, :], ugall[1, 4:5, :]], axis=1), (8, US)
    )
    q_c.wait_recv()
    q_f.wait_recv()
    for h in range(2):
        mask_users(1 - c, h)

    inv_t = 1.0 / jnp.full((8, US), t_ref[0], F32)
    inv_t16 = jnp.concatenate([inv_t, inv_t], axis=0)
    scale2 = inv_t * LOG2E
    row_iota = lax.broadcasted_iota(jnp.int32, (ROWS, US), 0)

    def twice(v):
        return jnp.concatenate([v, v], axis=0)

    def is_positive(o, r):
        ids = row_iota + ((o * 2 + c) * UB + x * CH + r * ROWS)
        return twice(tgtb[...]) == ids.astype(F32)

    def forward(j, carry):
        s = (j + 1) // 2
        odd = lax.rem(j, 2) == 1

        @pl.when(odd)
        def _():
            for hh in range(2):
                for n in range(2):
                    for dr in range(2):
                        last = 4 if hh == dr else 3

                        @pl.when(s <= last)
                        def _():
                            hop(dr, s, hh, n).wait_recv()

                        @pl.when(s < last)
                        def _():
                            hop(dr, s + 1, hh, n).start()

        o = lax.rem(z + NZ + jnp.where(odd, -s, s), NZ)
        gpad[0:16, :] = call[o, 0, CH:, :CH].astype(F32)
        gpad[16:32, :] = call[o, 1, CH:, :CH].astype(F32)
        git[...] = gpad[...].T * LOG2E
        for k in range(K):
            h, p = k // 4, (k % 4) // 2
            logit[o, k] = lax.dot_general(
                call[o, h, :CH, p * CH : (p + 1) * CH], qm[k], NT, preferred_element_type=F32
            )
        for h in range(2):
            for p in range(2):
                at = slice((2 * h + p) * CH, (2 * h + p + 1) * CH)
                ctall[o, at, :] = call[o, h, :CH, p * CH : (p + 1) * CH].T

        def rows_of(r, carry):
            top, pos = carry
            rows = pl.ds(pl.multiple_of(r * ROWS, ROWS), ROWS)
            den = num = None
            gcols = git[rows, :]
            for k in range(K):
                col = (k // 4) * 16 + k % 4
                l = logit[o, k, rows, :]
                e = jnp.tanh(l) * (slope_ref[k] * LOG2E) + gcols[:, col : col + 1] + twice(gub[k])
                w = jnp.exp2(e)
                weight[o, k, rows, :] = w
                wl = w * l
                den = w if den is None else den + w
                num = wl if num is None else num + wl
            di = 1.0 / den
            sc = num * di
            dinv[o, rows, :] = di
            score[o, rows, :] = sc
            hit = jnp.where(is_positive(o, r), sc, 0.0)
            return (
                jnp.maximum(top, jnp.maximum(sc[:8], sc[8:])),
                pos + hit[:8] + hit[8:],
            )

        before = mx[...]
        top, pos = lax.fori_loop(0, CH // ROWS, rows_of, (before, ps[...]))
        mx[...] = top
        ps[...] = pos
        shift = top * scale2
        total = sm[...] * jnp.exp2((before - top) * scale2)
        for m in range(CH // 8):
            total = total + jnp.exp2(score[o, m * 8 : (m + 1) * 8, :] * scale2 - shift)
        sm[...] = total
        return carry

    lax.fori_loop(0, NZ, forward, 0)

    top = jnp.max(mx[...], axis=0, keepdims=True)
    total = sm[...] * jnp.exp2((mx[...] - top) * scale2)
    stat[me] = jnp.concatenate(
        [
            top,
            jnp.sum(total, axis=0, keepdims=True),
            jnp.sum(ps[...], axis=0, keepdims=True),
            jnp.zeros((5, US), F32),
        ],
        axis=0,
    )
    st_sends = [rc(stat.at[me], stat.at[me], st_s.at[i], st_r.at[i], quad[i]) for i in range(3)]
    for s in st_sends:
        s.start()
    for s in st_sends:
        s.wait_recv()
    st = [stat[i] for i in range(4)]
    all_top = jnp.maximum(jnp.maximum(st[0][0:1], st[1][0:1]), jnp.maximum(st[2][0:1], st[3][0:1]))
    inv_row = inv_t[0:1]
    all_sum = all_pos = None
    for i in range(4):
        part = st[i][1:2] * jnp.exp((st[i][0:1] - all_top) * inv_row)
        all_sum = part if all_sum is None else all_sum + part
        all_pos = st[i][2:3] if all_pos is None else all_pos + st[i][2:3]
    log_total = all_top * inv_row + jnp.log(all_sum)
    loss = log_total - all_pos * inv_row
    loss_ref[...] = jnp.where(jnp.broadcast_to(c, (1, UB)) == 0, loss[:, :UB], loss[:, UB:])
    ltb[...] = jnp.broadcast_to(log_total * LOG2E, (8, US))

    ones_row = lax.broadcasted_iota(jnp.int32, (K, K * CH), 0)
    ones_col = lax.broadcasted_iota(jnp.int32, (K, K * CH), 1) // CH
    ones = jnp.where(ones_row == ones_col, 1.0, 0.0).astype(BF16)

    def gate_copy(dr, d):
        far = 2 if d in (2, 4) else 1
        return rc(
            gsend.at[dr, d - 1], grecv.at[dr, d - 1], g_s.at[dr, d - 1], g_r.at[dr, d - 1],
            dev(z + far * (2 * dr - 1), c, x),
        )

    def rs_copy(dr, d, h):
        far = 2 if d in (2, 4) else 1
        return rc(
            sbuf.at[dr, d - 1, h], rbuf.at[dr, d - 1, h], rs_s.at[dr, d - 1, h], rs_r.at[dr, d - 1, h],
            dev(z + far * (2 * dr - 1), c, x),
        )

    def last_copy(dr, w):
        h = x if w == 0 else 1 - x
        return rc(
            sbuf.at[dr, 0, h], rbuf.at[dr, 0, w], rs_s.at[dr, 0, w], rs_r.at[dr, 0, w],
            dev(z + 2 * dr - 1, c, h),
        )

    def far_of(j):
        d = 4 - (j + 1) // 2
        return d, lax.rem(z + NZ + jnp.where(lax.rem(j, 2) == 1, -d, d), NZ)

    def matmuls(o, b, k):
        ibk[k] = jnp.dot(lg[b, k], qm[k], preferred_element_type=F32)
        at = pl.ds(pl.multiple_of(k * 64, 64), 64)
        part = jnp.dot(ctall[o, at, :], lg[b, k], preferred_element_type=F32)
        uacc[0, at, :] += part[:, :UB]
        uacc[1, at, :] += part[:, UB:]

    def item_sum(h):
        return jnp.concatenate([ibk[4 * h] + ibk[4 * h + 1], ibk[4 * h + 2] + ibk[4 * h + 3]], axis=1)

    def backward(j, carry):
        d, o = far_of(j)
        before = jnp.maximum(j - 1, 0)
        d_before, o_before = far_of(before)
        b = lax.rem(j, 2)

        def rows_of(r, carry):
            rows = pl.ds(pl.multiple_of(r * ROWS, ROWS), ROWS)
            matmuls(o_before, 1 - b, r)
            sc = score[o, rows, :]
            soft = jnp.exp2(sc * twice(scale2) - twice(ltb[...]))
            soft = jnp.where(is_positive(o, r), soft - 1.0, soft) * inv_t16
            share = soft * dinv[o, rows, :]
            for k in range(K):
                l = logit[o, k, rows, :]
                t = jnp.tanh(l)
                g = weight[o, k, rows, :] * share
                gg = g * (l - sc)
                sk = slope_ref[k]
                out = g + gg * (sk - (t * t) * sk)
                lg[b, k, rows, :] = out.astype(BF16)
                ugv[k] = ugv[k] + (gg[:8] + gg[8:])
                igp[rows, k * CH : (k + 1) * CH] = (gg[:, 0:128] + gg[:, 128:256]) + (
                    gg[:, 256:384] + gg[:, 384:512]
                )
            return carry

        lax.fori_loop(0, CH // ROWS, rows_of, 0)

        dr_before = 1 - lax.rem(before, 2)

        @pl.when(j == 1)
        def _():
            for h in range(2):
                sbuf[h, 3, h] = item_sum(h).astype(BF16)
                rs_copy(h, 4, h).start()

        for dr in range(2):
            mine = (j > 1) & (dr_before == dr)

            @pl.when(mine & (d_before == 3))
            def _():
                for h in range(2):
                    sbuf[dr, 2, h] = item_sum(h).astype(BF16)
                    rs_copy(dr, 3, h).start()

            @pl.when(mine & (d_before == 2))
            def _():
                for h in range(2):
                    rs_copy(dr, 3, h).wait_recv()
                    value = item_sum(h) + rbuf[dr, 2, h].astype(F32)
                    if h == dr:
                        rs_copy(dr, 4, h).wait_recv()
                        value = value + rbuf[dr, 3, h].astype(F32)
                    sbuf[dr, 1, h] = value.astype(BF16)
                    rs_copy(dr, 2, h).start()

            @pl.when(mine & (d_before == 1))
            def _():
                for h in range(2):
                    sbuf[dr, 0, h] = item_sum(h).astype(BF16)
                for w in (1, 0):
                    last_copy(dr, w).start()

        hi = igp[...].astype(BF16)
        lo = (igp[...] - hi.astype(F32)).astype(BF16)
        gate = lax.dot_general(ones, hi, NT, preferred_element_type=F32) + lax.dot_general(
            ones, lo, NT, preferred_element_type=F32
        )

        @pl.when(j == 0)
        def _():
            gsend[0, 3] = gate
            gate_copy(0, 4).start()

        @pl.when(j == 7)
        def _():
            igx[0] = gate

        for dr in range(2):
            mine = (j > 0) & (j < 7) & (lax.rem(j, 2) == 1 - dr)
            for dd in (1, 3):

                @pl.when(mine & (d == dd))
                def _():
                    gsend[dr, dd - 1] = gate
                    gate_copy(dr, dd).start()

            @pl.when(mine & (d == 2))
            def _():
                gate_copy(dr, 3).wait_recv()
                value = gate + grecv[dr, 2]
                if dr == 0:
                    gate_copy(0, 4).wait_recv()
                    value = value + grecv[0, 3]
                gsend[dr, 1] = value
                gate_copy(dr, 2).start()

        return carry

    lax.fori_loop(0, NZ, backward, 0)

    for k in range(K):
        ugsend[k : k + 1, :] = jnp.sum(ugv[k], axis=0, keepdims=True)
    ug_sends = [rc(ugsend, ugrecv.at[i], ugs_s.at[i], ugs_r.at[i], quad[i]) for i in range(3)]
    for s in ug_sends:
        s.start()

    def u_core(hh, p):
        h = 1 - x if hh == 0 else x
        at = pl.ds(pl.multiple_of(h * UB + p * CH, CH), CH)
        return rc(uacc.at[1 - c, at, :], urecv.at[hh, p], uc_s.at[hh, p], uc_r.at[hh, p], cp)

    def u_x(p):
        return rc(usend.at[p], uxrecv.at[p], ux_s.at[p], ux_r.at[p], xp)

    def core_sum(hh, p):
        h = 1 - x if hh == 0 else x
        at = pl.ds(pl.multiple_of(h * UB + p * CH, CH), CH)
        u_core(hh, p).wait_recv()
        return uacc[c, at, :] + urecv[hh, p]

    for hh in range(2):
        for p in range(2):
            for kk in range(2):
                h = 1 - x if hh == 0 else x
                matmuls(z, 1, 4 * h + 2 * p + kk)
            u_core(hh, p).start()
    for p in range(2):
        usend[p] = core_sum(0, p).astype(BF16)
        u_x(p).start()

    def own_sum(h):
        for dr in range(2):
            rs_copy(dr, 2, h).wait_recv()
        return item_sum(h) + (rbuf[0, 1, h].astype(F32) + rbuf[1, 1, h].astype(F32))

    sums = [own_sum(h) for h in range(2)]
    first = jnp.broadcast_to(x, (CH, UB)) == 0
    isend[...] = jnp.where(first, sums[1], sums[0]).astype(BF16)
    keep = jnp.where(first, sums[0], sums[1])
    i_x = rc(isend, irecv, fx_s.at[0], fx_r.at[0], xp)
    i_x.start()
    gate = igx[0]
    for dr in range(2):
        for d in (2, 1):
            gate_copy(dr, d).wait_recv()
            gate = gate + grecv[dr, d - 1]
    igx[0] = gate
    ig_x = rc(igx.at[0], igx.at[1], fx_s.at[1], fx_r.at[1], xp)
    ig_x.start()

    for p in range(2):
        ukeep[p * CH : (p + 1) * CH, :] = core_sum(1, p)
    for s in ug_sends:
        s.wait_recv()
    ugate = (ugsend[...] + ugrecv[0]) + (ugrecv[1] + ugrecv[2])
    ugate = jnp.where(jnp.broadcast_to(c, (K, UB)) == 0, ugate[:, :UB], ugate[:, UB:])
    ugate_ref[...] = jnp.where(jnp.broadcast_to(x, (4, UB)) == 0, ugate[:4], ugate[4:])

    for dr in range(2):
        last_copy(dr, 0).wait_recv()
    ig_ref[own_rows, :] = keep + (rbuf[0, 0, 0].astype(F32) + rbuf[1, 0, 0].astype(F32))
    for dr in range(2):
        last_copy(dr, 1).wait_recv()
    i_x.wait_recv()
    ig_ref[peer_rows, :] = irecv[...].astype(F32) + (
        rbuf[0, 0, 1].astype(F32) + rbuf[1, 0, 1].astype(F32)
    )
    ig_x.wait_recv()
    mine, theirs = igx[0], igx[1]
    upper = jnp.concatenate([mine, theirs], axis=1)[:4]
    lower = jnp.concatenate([theirs, mine], axis=1)[4:]
    igate_ref[...] = jnp.where(jnp.broadcast_to(x, (4, UB)) == 0, upper, lower)
    for p in range(2):
        u_x(p).wait_recv()
        at = slice(p * CH, (p + 1) * CH)
        ug_ref[:, at] = (ukeep[at, :] + uxrecv[p].astype(F32)).T

    for s in (x_item, q_x, q_c, q_f, *u_sends, *st_sends, i_x, ig_x, *ug_sends):
        s.wait_send()
    for p in range(2):
        u_x(p).wait_send()
        for hh in range(2):
            u_core(hh, p).wait_send()
    gate_copy(0, 4).wait_send()
    for dr in range(2):
        rs_copy(dr, 4, dr).wait_send()
        for d in (1, 2, 3):
            gate_copy(dr, d).wait_send()
        for w in range(2):
            last_copy(dr, w).wait_send()
            for d in (2, 3):
                rs_copy(dr, d, w).wait_send()
        for hh in range(2):
            for s in range(1, 5 if hh == dr else 4):
                for n in range(2):
                    hop(dr, s, hh, n).wait_send()


def write_out(loss, ug, ig, ugate, igate, *outs):
    for a, o in zip((loss, ug, ig, ugate, igate), outs):
        o[...] = a[...]


def body(query, candidate, query_gate, candidate_gate, slope, scale, target):
    vmem = pl.BlockSpec(memory_space=pltpu.VMEM)
    smem = pl.BlockSpec(memory_space=pltpu.SMEM)
    dma = pltpu.SemaphoreType.DMA
    scratch = [
        pltpu.VMEM((2, 2, UB, UB), BF16),
        pltpu.VMEM((4, 8, UB), F32),
        pltpu.VMEM((NZ, 2, SLOT, UB), BF16),
        pltpu.VMEM((SLOT, UB), BF16),
        pltpu.VMEM((CH, CH), F32),
        pltpu.VMEM((CH, CH), F32),
        pltpu.VMEM((NZ, K * 64, CH), BF16),
        pltpu.VMEM((K, US, CH), BF16),
        pltpu.VMEM((K, 8, US), F32),
        pltpu.VMEM((8, US), F32),
        pltpu.VMEM((NZ, K, CH, US), F32),
        pltpu.VMEM((NZ, K, CH, US), F32),
        pltpu.VMEM((NZ, CH, US), F32),
        pltpu.VMEM((NZ, CH, US), F32),
        pltpu.VMEM((8, US), F32),
        pltpu.VMEM((8, US), F32),
        pltpu.VMEM((8, US), F32),
        pltpu.VMEM((4, 8, US), F32),
        pltpu.VMEM((8, US), F32),
        pltpu.VMEM((2, K, CH, US), BF16),
        pltpu.VMEM((CH, K * CH), F32),
        pltpu.VMEM((K, 8, US), F32),
        pltpu.VMEM((2, US, UB), F32),
        pltpu.VMEM((K, CH, CH), F32),
        pltpu.VMEM((2, 4, 2, CH, UB), BF16),
        pltpu.VMEM((2, 4, 2, CH, UB), BF16),
        pltpu.VMEM((2, 4, K, CH), F32),
        pltpu.VMEM((2, 4, K, CH), F32),
        pltpu.VMEM((2, 2, CH, UB), F32),
        pltpu.VMEM((UB, UB), F32),
        pltpu.VMEM((2, CH, UB), BF16),
        pltpu.VMEM((2, CH, UB), BF16),
        pltpu.VMEM((CH, UB), BF16),
        pltpu.VMEM((CH, UB), BF16),
        pltpu.VMEM((2, K, CH), F32),
        pltpu.VMEM((K, US), F32),
        pltpu.VMEM((3, K, US), F32),
        dma((1,)), dma((1,)),
        dma((3,)), dma((3,)),
        dma((3,)), dma((3,)),
        dma((2, 4, 2, 2)), dma((2, 4, 2, 2)),
        dma((3,)), dma((3,)),
        dma((2, 4, 2)), dma((2, 4, 2)),
        dma((2, 4)), dma((2, 4)),
        dma((2, 2)), dma((2, 2)),
        dma((2,)), dma((2,)),
        dma((2,)), dma((2,)),
        dma((3,)), dma((3,)),
    ]
    outs = (
        jax.ShapeDtypeStruct((1, UB), F32),
        jax.ShapeDtypeStruct((UB, UB), F32),
        jax.ShapeDtypeStruct((UB, UB), F32),
        jax.ShapeDtypeStruct((4, UB), F32),
        jax.ShapeDtypeStruct((4, UB), F32),
    )
    results = pl.pallas_call(
        kernel,
        out_shape=outs,
        in_specs=[vmem, vmem, vmem, vmem, smem, smem, vmem],
        out_specs=(vmem,) * 5,
        scratch_shapes=scratch,
        compiler_params=pltpu.CompilerParams(
            collective_id=0, has_side_effects=True, vmem_limit_bytes=60 * 1024 * 1024
        ),
    )(query, candidate, query_gate, candidate_gate, slope, scale, target.reshape(1, UB))
    loss, ug, ig, ugate, igate = pl.pallas_call(
        write_out, out_shape=outs, in_specs=[vmem] * 5, out_specs=(vmem,) * 5
    )(*results)
    return loss.reshape(UB), ug, ig, ugate, igate


def solution(mesh):
    in_specs = (
        P(("task", "blk"), "comp"),
        P(("task", "blk"), "comp"),
        P("comp", ("task", "blk")),
        P("comp", ("task", "blk")),
        P(),
        P("task"),
        P(("task", "blk")),
    )
    out_specs = (
        P(("task", "blk")),
        P(("task", "blk"), "comp"),
        P(("task", "blk"), "comp"),
        P("comp", ("task", "blk")),
        P("comp", ("task", "blk")),
    )
    return jax.shard_map(body, mesh=mesh, in_specs=in_specs, out_specs=out_specs, check_vma=False)
```

```python
import jax
import jax.numpy as jnp
from jax import lax
from jax.experimental import pallas as pl
from jax.experimental.pallas import tpu as pltpu
from jax.sharding import PartitionSpec as P

MESH = pl.DeviceIdType.MESH
LOG2E = 1.4426950408889634
F32, BF16 = jnp.float32, jnp.bfloat16
NZ = 8
UB = 256
US = 512
CH = 128
SLOT = CH + 16
PIECES = ((0, 80), (80, 64))
K = 8
ROWS = 16
BROWS = 32
NT = (((1,), (1,)), ((), ()))


def kernel(
    q_ref, c_ref, gq_ref, gc_ref, slope_ref, t_ref, tgt_ref,
    loss_ref, ug_ref, ig_ref, ugate_ref, igate_ref,
    qall, ugall, call, xstage, gpad, git, ctall, qm, gub, tgtb,
    logit, weight, score, dinv, mx, sm, ps, stat, ltb,
    lg_a, lg_b, igp_a, igp_b, gacc, ugv, uacc, ib, qpair, sbuf, rbuf, gsend, grecv,
    urecv, ukeep, usend, uxrecv, isend, irecv, igx, ugsend, ugrecv,
    x_s, x_r, q_s, q_r, u_s, u_r, ag_s, ag_r, st_s, st_r,
    rs_s, rs_r, g_s, g_r, uc_s, uc_r, ux_s, ux_r, fx_s, fx_r, ugs_s, ugs_r,
):
    blk = lax.axis_index("blk")
    x = lax.axis_index("comp")
    z = blk // 2
    c = lax.rem(blk, 2)
    me = 2 * x + c

    def dev(zz, cc, xx):
        return {"blk": lax.rem(zz + NZ, NZ) * 2 + cc, "comp": xx}

    def rc(src, dst, ss, rs, device):
        return pltpu.make_async_remote_copy(
            src_ref=src, dst_ref=dst, send_sem=ss, recv_sem=rs, device_id=device, device_id_type=MESH
        )

    xp, cp, dp = dev(z, c, 1 - x), dev(z, 1 - c, x), dev(z, 1 - c, 1 - x)
    quad = (xp, cp, dp)

    barrier = pltpu.get_barrier_semaphore()
    near = [dev(z + d, c, x) for d in (-2, -1, 1, 2)] + [dev(z + d, c, 1 - x) for d in (-1, 1)]
    for peer in (*quad, *near):
        pl.semaphore_signal(barrier, inc=1, device_id=peer, device_id_type=MESH)

    own_rows = pl.ds(pl.multiple_of(x * CH, CH), CH)
    peer_rows = pl.ds(pl.multiple_of((1 - x) * CH, CH), CH)
    gc = gc_ref[...].astype(F32)
    gc = jnp.concatenate([gc, gc], axis=0)
    gc = jnp.concatenate([gc, gc], axis=0)
    low = jnp.broadcast_to(x, (16, CH)) == 0
    blank = jnp.zeros((16, CH), F32)
    own_gate = jnp.concatenate([jnp.where(low, gc[:, :CH], gc[:, CH:]), blank], axis=1)
    peer_gate = jnp.concatenate([jnp.where(low, gc[:, CH:], gc[:, :CH]), blank], axis=1)
    call[z, x, :CH, :] = c_ref[own_rows, :]
    call[z, x, CH:, :] = own_gate.astype(BF16)
    xstage[:CH, :] = c_ref[peer_rows, :]
    xstage[CH:, :] = peer_gate.astype(BF16)
    qall[c, x] = q_ref[...]
    gq = gq_ref[...].astype(F32)
    ugall[me] = jnp.concatenate([gq, jnp.broadcast_to(tgt_ref[...].astype(F32), (4, UB))], axis=0)

    pl.semaphore_wait(barrier, len(quad) + len(near))

    def hop(dr, s, hh, n):
        step = 1 - 2 * dr
        o = lax.rem(z - step * (s - 1) + NZ, NZ)
        h = x if hh == 0 else 1 - x
        at = call.at[o, h, pl.ds(*PIECES[n]), :]
        return rc(at, at, ag_s.at[dr, s - 1, hh, n], ag_r.at[dr, s - 1, hh, n], dev(z + step, c, x))

    x_item = rc(xstage, call.at[z, x], x_s.at[0], x_r.at[0], xp)
    q_x = rc(q_ref, qall.at[c, x], q_s.at[0], q_r.at[0], xp)
    q_c = rc(q_ref, qall.at[c, x], q_s.at[1], q_r.at[1], cp)
    q_f = rc(qall.at[c, 1 - x], qall.at[c, 1 - x], q_s.at[2], q_r.at[2], cp)
    u_sends = [rc(ugall.at[me], ugall.at[me], u_s.at[i], u_r.at[i], quad[i]) for i in range(3)]
    x_item.start()
    for n in range(2):
        hop(0, 1, 0, n).start()
        hop(1, 1, 0, n).start()
    q_x.start()
    for s in u_sends:
        s.start()
    q_c.start()

    gpad[...] = jnp.zeros_like(gpad)
    mx[...] = jnp.full(mx.shape, -3.0e38, F32)
    sm[...] = jnp.zeros_like(sm)
    ps[...] = jnp.zeros_like(ps)
    uacc[...] = jnp.zeros_like(uacc)
    ugv[...] = jnp.zeros_like(ugv)
    lg_b[...] = jnp.zeros_like(lg_b)
    igp_b[...] = jnp.zeros_like(igp_b)

    x_item.wait_recv()
    for n in range(2):
        hop(0, 1, 1, n).start()
        hop(1, 1, 1, n).start()
    q_x.wait_recv()
    q_f.start()

    lane = lax.broadcasted_iota(jnp.int32, (UB, CH), 1)

    def mask_users(cc, h):
        for p in range(2):
            rows = pl.ds(pl.multiple_of(cc * UB, UB), UB)
            k = 4 * h + 2 * p
            qpair[k // 2, rows, :] = qall[cc, h, :, p * CH : (p + 1) * CH]
            pair = qall[cc, h, :, p * CH : (p + 1) * CH].astype(F32)
            qm[k, rows, :] = jnp.where(lane < 64, pair, 0.0).astype(BF16)
            qm[k + 1, rows, :] = jnp.where(lane < 64, 0.0, pair).astype(BF16)

    for h in range(2):
        mask_users(c, h)
    for s in u_sends:
        s.wait_recv()
    for k in range(K):
        h, r = k // 4, k % 4
        row = jnp.concatenate([ugall[2 * h, r : r + 1, :], ugall[2 * h + 1, r : r + 1, :]], axis=1)
        gub[k] = jnp.broadcast_to(row * LOG2E, (8, US))
    tgtb[...] = jnp.broadcast_to(
        jnp.concatenate([ugall[0, 4:5, :], ugall[1, 4:5, :]], axis=1), (8, US)
    )
    q_c.wait_recv()
    q_f.wait_recv()
    for h in range(2):
        mask_users(1 - c, h)

    inv_t = 1.0 / jnp.full((8, US), t_ref[0], F32)
    scale2 = inv_t * LOG2E

    def twice(v):
        return jnp.concatenate([v, v], axis=0)

    def is_positive(o, r, rows):
        ids = lax.broadcasted_iota(jnp.int32, (rows, US), 0) + (
            (o * 2 + c) * UB + x * CH + r * rows
        )
        return jnp.concatenate([tgtb[...]] * (rows // 8), axis=0) == ids.astype(F32)

    def forward(j, carry):
        s = (j + 1) // 2
        odd = lax.rem(j, 2) == 1

        @pl.when(odd)
        def _():
            for hh in range(2):
                for n in range(2):
                    for dr in range(2):
                        last = 4 if hh == dr else 3

                        @pl.when(s <= last)
                        def _():
                            hop(dr, s, hh, n).wait_recv()

                        @pl.when(s < last)
                        def _():
                            hop(dr, s + 1, hh, n).start()

        o = lax.rem(z + NZ + jnp.where(odd, -s, s), NZ)
        gpad[0:16, :] = call[o, 0, CH:, :CH].astype(F32)
        gpad[16:32, :] = call[o, 1, CH:, :CH].astype(F32)
        git[...] = gpad[...].T * LOG2E
        for k in range(K):
            h, p = k // 4, (k % 4) // 2
            logit[o, k] = lax.dot_general(
                call[o, h, :CH, p * CH : (p + 1) * CH], qm[k], NT, preferred_element_type=F32
            )
        for h in range(2):
            for p in range(2):
                at = slice((2 * h + p) * CH, (2 * h + p + 1) * CH)
                ctall[o, at, :] = call[o, h, :CH, p * CH : (p + 1) * CH].T

        def rows_of(r, carry):
            top, pos = carry
            rows = pl.ds(pl.multiple_of(r * ROWS, ROWS), ROWS)
            den = num = None
            gcols = git[rows, :]
            for k in range(K):
                col = (k // 4) * 16 + k % 4
                l = logit[o, k, rows, :]
                e = jnp.tanh(l) * (slope_ref[k] * LOG2E) + gcols[:, col : col + 1] + twice(gub[k])
                w = jnp.exp2(e)
                weight[o, k, rows, :] = w
                wl = w * l
                den = w if den is None else den + w
                num = wl if num is None else num + wl
            di = 1.0 / den
            sc = num * di
            dinv[o, rows, :] = di
            score[o, rows, :] = sc
            hit = jnp.where(is_positive(o, r, ROWS), sc, 0.0)
            return (
                jnp.maximum(top, jnp.maximum(sc[:8], sc[8:])),
                pos + hit[:8] + hit[8:],
            )

        before = mx[...]
        top, pos = lax.fori_loop(0, CH // ROWS, rows_of, (before, ps[...]))
        mx[...] = top
        ps[...] = pos
        shift = top * scale2
        total = sm[...] * jnp.exp2((before - top) * scale2)
        for m in range(CH // 8):
            total = total + jnp.exp2(score[o, m * 8 : (m + 1) * 8, :] * scale2 - shift)
        sm[...] = total
        return carry

    lax.fori_loop(0, NZ, forward, 0)

    top = jnp.max(mx[...], axis=0, keepdims=True)
    total = sm[...] * jnp.exp2((mx[...] - top) * scale2)
    stat[me] = jnp.concatenate(
        [
            top,
            jnp.sum(total, axis=0, keepdims=True),
            jnp.sum(ps[...], axis=0, keepdims=True),
            jnp.zeros((5, US), F32),
        ],
        axis=0,
    )
    st_sends = [rc(stat.at[me], stat.at[me], st_s.at[i], st_r.at[i], quad[i]) for i in range(3)]
    for s in st_sends:
        s.start()
    for s in st_sends:
        s.wait_recv()
    st = [stat[i] for i in range(4)]
    all_top = jnp.maximum(jnp.maximum(st[0][0:1], st[1][0:1]), jnp.maximum(st[2][0:1], st[3][0:1]))
    inv_row = inv_t[0:1]
    all_sum = all_pos = None
    for i in range(4):
        part = st[i][1:2] * jnp.exp((st[i][0:1] - all_top) * inv_row)
        all_sum = part if all_sum is None else all_sum + part
        all_pos = st[i][2:3] if all_pos is None else all_pos + st[i][2:3]
    log_total = all_top * inv_row + jnp.log(all_sum)
    loss = log_total - all_pos * inv_row
    loss_ref[...] = jnp.where(jnp.broadcast_to(c, (1, UB)) == 0, loss[:, :UB], loss[:, UB:])
    ltb[...] = jnp.broadcast_to(log_total * LOG2E, (8, US))

    ones_row = lax.broadcasted_iota(jnp.int32, (8, 2 * CH), 0)
    ones_col = lax.broadcasted_iota(jnp.int32, (8, 2 * CH), 1) // CH
    ones = jnp.where(ones_row == ones_col, 1.0, 0.0).astype(BF16)

    def gate_copy(dr, d):
        far = 2 if d in (2, 4) else 1
        return rc(
            gsend.at[dr, d - 1], grecv.at[dr, d - 1], g_s.at[dr, d - 1], g_r.at[dr, d - 1],
            dev(z + far * (2 * dr - 1), c, x),
        )

    def rs_copy(dr, d, h):
        far = 2 if d in (2, 4) else 1
        return rc(
            sbuf.at[dr, d - 1, h], rbuf.at[dr, d - 1, h], rs_s.at[dr, d - 1, h], rs_r.at[dr, d - 1, h],
            dev(z + far * (2 * dr - 1), c, x),
        )

    def last_copy(dr, w):
        h = x if w == 0 else 1 - x
        return rc(
            sbuf.at[dr, 0, h], rbuf.at[dr, 0, w], rs_s.at[dr, 0, w], rs_r.at[dr, 0, w],
            dev(z + 2 * dr - 1, c, h),
        )

    def matmuls(o, lg, igp, r):
        both = jnp.dot(
            lg[pl.ds(pl.multiple_of(r * 2 * CH, 2 * CH), 2 * CH), :], qpair[r], preferred_element_type=F32
        )
        ib[r] = jnp.where(lane[:CH] < 64, both[:CH], both[CH:])
        for kk in range(2):
            at = pl.ds(pl.multiple_of(r * CH + kk * 64, 64), 64)
            part = jnp.dot(
                ctall[o, at, :],
                lg[pl.ds(pl.multiple_of((2 * r + kk) * CH, CH), CH), :],
                preferred_element_type=F32,
            )
            uacc[0, at, :] += part[:, :UB]
            uacc[1, at, :] += part[:, UB:]
        gates = igp[r]
        hi = gates.astype(BF16)
        lo = (gates - hi.astype(F32)).astype(BF16)
        gacc[r] = lax.dot_general(ones, hi, NT, preferred_element_type=F32) + lax.dot_general(
            ones, lo, NT, preferred_element_type=F32
        )

    def item_sum(h):
        return jnp.concatenate([ib[2 * h], ib[2 * h + 1]], axis=1)

    def gate_sum():
        return jnp.concatenate([gacc[i, 0:2, :] for i in range(4)], axis=0)

    def four(v):
        return jnp.concatenate([v] * (BROWS // 8), axis=0)

    def chunk(o, lg, igp, o_before, lg_before, igp_before):
        def rows_of(r, carry):
            rows = pl.ds(pl.multiple_of(r * BROWS, BROWS), BROWS)
            matmuls(o_before, lg_before, igp_before, r)
            sc = score[o, rows, :]
            soft = jnp.exp2(sc * four(scale2) - four(ltb[...]))
            soft = jnp.where(is_positive(o, r, BROWS), soft - 1.0, soft) * four(inv_t)
            share = soft * dinv[o, rows, :]
            for k in range(K):
                l = logit[o, k, rows, :]
                t = jnp.tanh(l)
                g = weight[o, k, rows, :] * share
                gg = g * (l - sc)
                sk = slope_ref[k]
                out = g + gg * (sk - (t * t) * sk)
                lg[pl.ds(pl.multiple_of(k * CH + r * BROWS, BROWS), BROWS), :] = out.astype(BF16)
                ugv[k] = ugv[k] + ((gg[:8] + gg[8:16]) + (gg[16:24] + gg[24:]))
                igp[k // 2, rows, (k % 2) * CH : (k % 2 + 1) * CH] = (
                    gg[:, 0:128] + gg[:, 128:256]
                ) + (gg[:, 256:384] + gg[:, 384:512])
            return carry

        lax.fori_loop(0, CH // BROWS, rows_of, 0)

    def send(dr, jj):
        @pl.when(jj == 1)
        def _():
            for h in range(2):
                sbuf[dr, 2, h] = item_sum(h).astype(BF16)
                rs_copy(dr, 3, h).start()
            gsend[dr, 2] = gate_sum()
            gate_copy(dr, 3).start()

        @pl.when(jj == 2)
        def _():
            for h in range(2):
                rs_copy(dr, 3, h).wait_recv()
                value = item_sum(h) + rbuf[dr, 2, h].astype(F32)
                if h == dr:
                    rs_copy(dr, 4, h).wait_recv()
                    value = value + rbuf[dr, 3, h].astype(F32)
                sbuf[dr, 1, h] = value.astype(BF16)
                rs_copy(dr, 2, h).start()
            gate_copy(dr, 3).wait_recv()
            value = gate_sum() + grecv[dr, 2]
            if dr == 0:
                gate_copy(0, 4).wait_recv()
                value = value + grecv[0, 3]
            gsend[dr, 1] = value
            gate_copy(dr, 2).start()

        @pl.when(jj == 3)
        def _():
            for h in range(2):
                sbuf[dr, 0, h] = item_sum(h).astype(BF16)
            for w in (1, 0):
                last_copy(dr, w).start()
            gsend[dr, 0] = gate_sum()
            gate_copy(dr, 1).start()

    def backward(jj, carry):
        d = 4 - jj
        right = lax.rem(z + d, NZ)
        chunk(right, lg_a, igp_a, lax.rem(z + NZ - d, NZ), lg_b, igp_b)
        send(0, jj)
        chunk(lax.rem(z + NZ - (d - 1), NZ), lg_b, igp_b, right, lg_a, igp_a)

        @pl.when(jj == 0)
        def _():
            for h in range(2):
                sbuf[h, 3, h] = item_sum(h).astype(BF16)
                rs_copy(h, 4, h).start()
            gsend[0, 3] = gate_sum()
            gate_copy(0, 4).start()

        send(1, jj)
        return carry

    lax.fori_loop(0, NZ // 2, backward, 0)

    for k in range(K):
        ugsend[k : k + 1, :] = jnp.sum(ugv[k], axis=0, keepdims=True)
    ug_sends = [rc(ugsend, ugrecv.at[i], ugs_s.at[i], ugs_r.at[i], quad[i]) for i in range(3)]
    for s in ug_sends:
        s.start()

    def u_core(hh, p):
        h = 1 - x if hh == 0 else x
        at = pl.ds(pl.multiple_of(h * UB + p * CH, CH), CH)
        return rc(uacc.at[1 - c, at, :], urecv.at[hh, p], uc_s.at[hh, p], uc_r.at[hh, p], cp)

    def u_x(p):
        return rc(usend.at[p], uxrecv.at[p], ux_s.at[p], ux_r.at[p], xp)

    def core_sum(hh, p):
        h = 1 - x if hh == 0 else x
        at = pl.ds(pl.multiple_of(h * UB + p * CH, CH), CH)
        u_core(hh, p).wait_recv()
        return uacc[c, at, :] + urecv[hh, p]

    for hh in range(2):
        for p in range(2):
            h = 1 - x if hh == 0 else x
            matmuls(z, lg_b, igp_b, 2 * h + p)
            u_core(hh, p).start()
    for p in range(2):
        usend[p] = core_sum(0, p).astype(BF16)
        u_x(p).start()

    def own_sum(h):
        for dr in range(2):
            rs_copy(dr, 2, h).wait_recv()
        return item_sum(h) + (rbuf[0, 1, h].astype(F32) + rbuf[1, 1, h].astype(F32))

    sums = [own_sum(h) for h in range(2)]
    first = jnp.broadcast_to(x, (CH, UB)) == 0
    isend[...] = jnp.where(first, sums[1], sums[0]).astype(BF16)
    keep = jnp.where(first, sums[0], sums[1])
    i_x = rc(isend, irecv, fx_s.at[0], fx_r.at[0], xp)
    i_x.start()
    gate = gate_sum()
    for dr in range(2):
        for d in (2, 1):
            gate_copy(dr, d).wait_recv()
            gate = gate + grecv[dr, d - 1]
    igx[0] = gate
    ig_x = rc(igx.at[0], igx.at[1], fx_s.at[1], fx_r.at[1], xp)
    ig_x.start()

    for p in range(2):
        ukeep[p * CH : (p + 1) * CH, :] = core_sum(1, p)
    for s in ug_sends:
        s.wait_recv()
    ugate = (ugsend[...] + ugrecv[0]) + (ugrecv[1] + ugrecv[2])
    ugate = jnp.where(jnp.broadcast_to(c, (K, UB)) == 0, ugate[:, :UB], ugate[:, UB:])
    ugate_ref[...] = jnp.where(jnp.broadcast_to(x, (4, UB)) == 0, ugate[:4], ugate[4:])

    for dr in range(2):
        last_copy(dr, 0).wait_recv()
    ig_ref[own_rows, :] = keep + (rbuf[0, 0, 0].astype(F32) + rbuf[1, 0, 0].astype(F32))
    for dr in range(2):
        last_copy(dr, 1).wait_recv()
    i_x.wait_recv()
    ig_ref[peer_rows, :] = irecv[...].astype(F32) + (
        rbuf[0, 0, 1].astype(F32) + rbuf[1, 0, 1].astype(F32)
    )
    ig_x.wait_recv()
    mine, theirs = igx[0], igx[1]
    upper = jnp.concatenate([mine, theirs], axis=1)[:4]
    lower = jnp.concatenate([theirs, mine], axis=1)[4:]
    igate_ref[...] = jnp.where(jnp.broadcast_to(x, (4, UB)) == 0, upper, lower)
    for p in range(2):
        u_x(p).wait_recv()
        at = slice(p * CH, (p + 1) * CH)
        ug_ref[:, at] = (ukeep[at, :] + uxrecv[p].astype(F32)).T

    for s in (x_item, q_x, q_c, q_f, *u_sends, *st_sends, i_x, ig_x, *ug_sends):
        s.wait_send()
    for p in range(2):
        u_x(p).wait_send()
        for hh in range(2):
            u_core(hh, p).wait_send()
    gate_copy(0, 4).wait_send()
    for dr in range(2):
        rs_copy(dr, 4, dr).wait_send()
        for d in (1, 2, 3):
            gate_copy(dr, d).wait_send()
        for w in range(2):
            last_copy(dr, w).wait_send()
            for d in (2, 3):
                rs_copy(dr, d, w).wait_send()
        for hh in range(2):
            for s in range(1, 5 if hh == dr else 4):
                for n in range(2):
                    hop(dr, s, hh, n).wait_send()


def write_out(loss, ug, ig, ugate, igate, *outs):
    for a, o in zip((loss, ug, ig, ugate, igate), outs):
        o[...] = a[...]


def body(query, candidate, query_gate, candidate_gate, slope, scale, target):
    vmem = pl.BlockSpec(memory_space=pltpu.VMEM)
    smem = pl.BlockSpec(memory_space=pltpu.SMEM)
    dma = pltpu.SemaphoreType.DMA
    scratch = [
        pltpu.VMEM((2, 2, UB, UB), BF16),
        pltpu.VMEM((4, 8, UB), F32),
        pltpu.VMEM((NZ, 2, SLOT, UB), BF16),
        pltpu.VMEM((SLOT, UB), BF16),
        pltpu.VMEM((CH, CH), F32),
        pltpu.VMEM((CH, CH), F32),
        pltpu.VMEM((NZ, K * 64, CH), BF16),
        pltpu.VMEM((K, US, CH), BF16),
        pltpu.VMEM((K, 8, US), F32),
        pltpu.VMEM((8, US), F32),
        pltpu.VMEM((NZ, K, CH, US), F32),
        pltpu.VMEM((NZ, K, CH, US), F32),
        pltpu.VMEM((NZ, CH, US), F32),
        pltpu.VMEM((NZ, CH, US), F32),
        pltpu.VMEM((8, US), F32),
        pltpu.VMEM((8, US), F32),
        pltpu.VMEM((8, US), F32),
        pltpu.VMEM((4, 8, US), F32),
        pltpu.VMEM((8, US), F32),
        pltpu.VMEM((K * CH, US), BF16),
        pltpu.VMEM((K * CH, US), BF16),
        pltpu.VMEM((4, CH, 2 * CH), F32),
        pltpu.VMEM((4, CH, 2 * CH), F32),
        pltpu.VMEM((4, 8, CH), F32),
        pltpu.VMEM((K, 8, US), F32),
        pltpu.VMEM((2, US, UB), F32),
        pltpu.VMEM((4, CH, CH), F32),
        pltpu.VMEM((4, US, CH), BF16),
        pltpu.VMEM((2, 4, 2, CH, UB), BF16),
        pltpu.VMEM((2, 4, 2, CH, UB), BF16),
        pltpu.VMEM((2, 4, K, CH), F32),
        pltpu.VMEM((2, 4, K, CH), F32),
        pltpu.VMEM((2, 2, CH, UB), F32),
        pltpu.VMEM((UB, UB), F32),
        pltpu.VMEM((2, CH, UB), BF16),
        pltpu.VMEM((2, CH, UB), BF16),
        pltpu.VMEM((CH, UB), BF16),
        pltpu.VMEM((CH, UB), BF16),
        pltpu.VMEM((2, K, CH), F32),
        pltpu.VMEM((K, US), F32),
        pltpu.VMEM((3, K, US), F32),
        dma((1,)), dma((1,)),
        dma((3,)), dma((3,)),
        dma((3,)), dma((3,)),
        dma((2, 4, 2, 2)), dma((2, 4, 2, 2)),
        dma((3,)), dma((3,)),
        dma((2, 4, 2)), dma((2, 4, 2)),
        dma((2, 4)), dma((2, 4)),
        dma((2, 2)), dma((2, 2)),
        dma((2,)), dma((2,)),
        dma((2,)), dma((2,)),
        dma((3,)), dma((3,)),
    ]
    outs = (
        jax.ShapeDtypeStruct((1, UB), F32),
        jax.ShapeDtypeStruct((UB, UB), F32),
        jax.ShapeDtypeStruct((UB, UB), F32),
        jax.ShapeDtypeStruct((4, UB), F32),
        jax.ShapeDtypeStruct((4, UB), F32),
    )
    results = pl.pallas_call(
        kernel,
        out_shape=outs,
        in_specs=[vmem, vmem, vmem, vmem, smem, smem, vmem],
        out_specs=(vmem,) * 5,
        scratch_shapes=scratch,
        compiler_params=pltpu.CompilerParams(
            collective_id=0, has_side_effects=True, vmem_limit_bytes=60 * 1024 * 1024
        ),
    )(query, candidate, query_gate, candidate_gate, slope, scale, target.reshape(1, UB))
    loss, ug, ig, ugate, igate = pl.pallas_call(
        write_out, out_shape=outs, in_specs=[vmem] * 5, out_specs=(vmem,) * 5
    )(*results)
    return loss.reshape(UB), ug, ig, ugate, igate


def solution(mesh):
    in_specs = (
        P(("task", "blk"), "comp"),
        P(("task", "blk"), "comp"),
        P("comp", ("task", "blk")),
        P("comp", ("task", "blk")),
        P(),
        P("task"),
        P(("task", "blk")),
    )
    out_specs = (
        P(("task", "blk")),
        P(("task", "blk"), "comp"),
        P(("task", "blk"), "comp"),
        P("comp", ("task", "blk")),
        P("comp", ("task", "blk")),
    )
    return jax.shard_map(body, mesh=mesh, in_specs=in_specs, out_specs=out_specs, check_vma=False)
```

```python
import jax
import jax.numpy as jnp
from jax import lax
from jax.experimental import pallas as pl
from jax.experimental.pallas import tpu as pltpu
from jax.sharding import PartitionSpec as P

MESH = pl.DeviceIdType.MESH
LOG2E = 1.4426950408889634
F32, BF16 = jnp.float32, jnp.bfloat16
NZ = 8
UB = 256
US = 512
CH = 128
SLOT = CH + 16
PIECES = ((0, 80), (80, 64))
K = 8
ROWS = 16
BROWS = 32
NT = (((1,), (1,)), ((), ()))


def kernel(
    q_ref, c_ref, gq_ref, gc_ref, slope_ref, t_ref, tgt_ref,
    loss_ref, ug_ref, ig_ref, ugate_ref, igate_ref,
    qall, ugall, call, xstage, gpad_a, gpad_b, git_a, git_b, ctall, qm, gub, tgtb,
    logit_a, logit_b, weight, score, dinv, mx, sm, ps, stat, ltb,
    lg_a, lg_b, igp_a, igp_b, gacc, ugv, uacc, ib, qpair, sbuf, rbuf, gsend, grecv,
    urecv, ukeep, usend, uxrecv, isend, irecv, igx, ugsend, ugrecv,
    x_s, x_r, q_s, q_r, u_s, u_r, ag_s, ag_r, st_s, st_r,
    rs_s, rs_r, g_s, g_r, uc_s, uc_r, ux_s, ux_r, fx_s, fx_r, ugs_s, ugs_r,
):
    blk = lax.axis_index("blk")
    x = lax.axis_index("comp")
    z = blk // 2
    c = lax.rem(blk, 2)
    me = 2 * x + c

    def dev(zz, cc, xx):
        return {"blk": lax.rem(zz + NZ, NZ) * 2 + cc, "comp": xx}

    def rc(src, dst, ss, rs, device):
        return pltpu.make_async_remote_copy(
            src_ref=src, dst_ref=dst, send_sem=ss, recv_sem=rs, device_id=device, device_id_type=MESH
        )

    xp, cp, dp = dev(z, c, 1 - x), dev(z, 1 - c, x), dev(z, 1 - c, 1 - x)
    quad = (xp, cp, dp)

    barrier = pltpu.get_barrier_semaphore()
    near = [dev(z + d, c, x) for d in (-2, -1, 1, 2)] + [dev(z + d, c, 1 - x) for d in (-1, 1)]
    for peer in (*quad, *near):
        pl.semaphore_signal(barrier, inc=1, device_id=peer, device_id_type=MESH)

    own_rows = pl.ds(pl.multiple_of(x * CH, CH), CH)
    peer_rows = pl.ds(pl.multiple_of((1 - x) * CH, CH), CH)
    gc = gc_ref[...].astype(F32)
    gc = jnp.concatenate([gc, gc], axis=0)
    gc = jnp.concatenate([gc, gc], axis=0)
    low = jnp.broadcast_to(x, (16, CH)) == 0
    blank = jnp.zeros((16, CH), F32)
    own_gate = jnp.concatenate([jnp.where(low, gc[:, :CH], gc[:, CH:]), blank], axis=1)
    peer_gate = jnp.concatenate([jnp.where(low, gc[:, CH:], gc[:, :CH]), blank], axis=1)
    call[z, x, :CH, :] = c_ref[own_rows, :]
    call[z, x, CH:, :] = own_gate.astype(BF16)
    xstage[:CH, :] = c_ref[peer_rows, :]
    xstage[CH:, :] = peer_gate.astype(BF16)
    qall[c, x] = q_ref[...]
    gq = gq_ref[...].astype(F32)
    ugall[me] = jnp.concatenate([gq, jnp.broadcast_to(tgt_ref[...].astype(F32), (4, UB))], axis=0)

    pl.semaphore_wait(barrier, len(quad) + len(near))

    def hop(dr, s, hh, n):
        step = 1 - 2 * dr
        o = lax.rem(z - step * min(s - 1, 2) + NZ, NZ)
        h = x if hh == 0 else 1 - x
        at = call.at[o, h, pl.ds(*PIECES[n]), :]
        return rc(at, at, ag_s.at[dr, s - 1, hh, n], ag_r.at[dr, s - 1, hh, n],
                  dev(z + (2 * step if s == 4 else step), c, x))

    def arrive(s, halves=(0, 1)):
        for hh in halves:
            for n in range(2):
                for dr in range(2):
                    if s < 4 or hh == dr:
                        hop(dr, s, hh, n).wait_recv()
                    if s == 2 and hh == dr:
                        hop(dr, 4, hh, n).start()
                    if s < 3:
                        hop(dr, s + 1, hh, n).start()

    x_item = rc(xstage, call.at[z, x], x_s.at[0], x_r.at[0], xp)
    q_x = rc(q_ref, qall.at[c, x], q_s.at[0], q_r.at[0], xp)
    q_c = rc(q_ref, qall.at[c, x], q_s.at[1], q_r.at[1], cp)
    q_f = rc(qall.at[c, 1 - x], qall.at[c, 1 - x], q_s.at[2], q_r.at[2], cp)
    u_sends = [rc(ugall.at[me], ugall.at[me], u_s.at[i], u_r.at[i], quad[i]) for i in range(3)]
    x_item.start()
    for n in range(2):
        hop(0, 1, 0, n).start()
        hop(1, 1, 0, n).start()
    q_x.start()
    for s in u_sends:
        s.start()
    q_c.start()

    gpad_a[...] = jnp.zeros_like(gpad_a)
    gpad_b[...] = jnp.zeros_like(gpad_b)
    mx[...] = jnp.full(mx.shape, -3.0e38, F32)
    sm[...] = jnp.zeros_like(sm)
    ps[...] = jnp.zeros_like(ps)
    uacc[...] = jnp.zeros_like(uacc)
    ugv[...] = jnp.zeros_like(ugv)
    lg_b[...] = jnp.zeros_like(lg_b)
    igp_b[...] = jnp.zeros_like(igp_b)

    x_item.wait_recv()
    for n in range(2):
        hop(0, 1, 1, n).start()
        hop(1, 1, 1, n).start()
    q_x.wait_recv()
    q_f.start()
    arrive(1, (0,))

    lane = lax.broadcasted_iota(jnp.int32, (UB, CH), 1)

    def mask_users(cc, h):
        for p in range(2):
            rows = pl.ds(pl.multiple_of(cc * UB, UB), UB)
            k = 4 * h + 2 * p
            qpair[k // 2, rows, :] = qall[cc, h, :, p * CH : (p + 1) * CH]
            pair = qall[cc, h, :, p * CH : (p + 1) * CH].astype(F32)
            qm[k, rows, :] = jnp.where(lane < 64, pair, 0.0).astype(BF16)
            qm[k + 1, rows, :] = jnp.where(lane < 64, 0.0, pair).astype(BF16)

    for h in range(2):
        mask_users(c, h)
    for s in u_sends:
        s.wait_recv()
    for k in range(K):
        h, r = k // 4, k % 4
        row = jnp.concatenate([ugall[2 * h, r : r + 1, :], ugall[2 * h + 1, r : r + 1, :]], axis=1)
        gub[k] = jnp.broadcast_to(row * LOG2E, (8, US))
    tgtb[...] = jnp.broadcast_to(
        jnp.concatenate([ugall[0, 4:5, :], ugall[1, 4:5, :]], axis=1), (8, US)
    )
    q_c.wait_recv()
    q_f.wait_recv()
    for h in range(2):
        mask_users(1 - c, h)

    inv_t = 1.0 / jnp.full((8, US), t_ref[0], F32)
    scale2 = inv_t * LOG2E

    def twice(v):
        return jnp.concatenate([v, v], axis=0)

    def is_positive(o, r, rows):
        ids = lax.broadcasted_iota(jnp.int32, (rows, US), 0) + (
            (o * 2 + c) * UB + x * CH + r * rows
        )
        return jnp.concatenate([tgtb[...]] * (rows // 8), axis=0) == ids.astype(F32)

    def gates_of(o, gpad, git):
        gpad[0:16, :] = call[o, 0, CH:, :CH].astype(F32)
        gpad[16:32, :] = call[o, 1, CH:, :CH].astype(F32)
        git[...] = gpad[...].T * LOG2E

    def logits_of(o, logit, s, k):
        h, p = k // 4, lax.rem(k, 4) // 2
        at = pl.ds(pl.multiple_of(p * CH, CH), CH)
        logit[s, k] = lax.dot_general(call[o, h, :CH, at], qm[k], NT, preferred_element_type=F32)

    def scores_of(o, logit, s, git, o_next, logit_next, s_next, gpad_next, git_next):
        gates_of(o_next, gpad_next, git_next)
        for h in range(2):
            for p in range(2):
                at = slice((2 * h + p) * CH, (2 * h + p + 1) * CH)
                ctall[o, at, :] = call[o, h, :CH, p * CH : (p + 1) * CH].T

        def rows_of(r, carry):
            top, pos = carry
            logits_of(o_next, logit_next, s_next, r)
            rows = pl.ds(pl.multiple_of(r * ROWS, ROWS), ROWS)
            den = num = None
            gcols = git[rows, :]
            for k in range(K):
                col = (k // 4) * 16 + k % 4
                l = logit[s, k, rows, :]
                e = jnp.tanh(l) * (slope_ref[k] * LOG2E) + gcols[:, col : col + 1] + twice(gub[k])
                w = jnp.exp2(e)
                weight[o, k, rows, :] = w
                wl = w * l
                den = w if den is None else den + w
                num = wl if num is None else num + wl
            di = 1.0 / den
            sc = num * di
            dinv[o, rows, :] = di
            score[o, rows, :] = sc
            hit = jnp.where(is_positive(o, r, ROWS), sc, 0.0)
            return (
                jnp.maximum(top, jnp.maximum(sc[:8], sc[8:])),
                pos + hit[:8] + hit[8:],
            )

        before = mx[...]
        top, pos = lax.fori_loop(0, CH // ROWS, rows_of, (before, ps[...]), unroll=True)
        mx[...] = top
        ps[...] = pos
        shift = top * scale2
        total = sm[...] * jnp.exp2((before - top) * scale2)
        for m in range(CH // 8):
            total = total + jnp.exp2(score[o, m * 8 : (m + 1) * 8, :] * scale2 - shift)
        sm[...] = total

    arrive(1, (1,))
    gates_of(z, gpad_a, git_a)

    def own_logits(k, carry):
        logits_of(z, logit_a, 0, k)
        return carry

    lax.fori_loop(0, K, own_logits, 0, unroll=True)

    def forward(i, carry):
        for s in (2, 3, 4):

            @pl.when(i == s - 1)
            def _():
                arrive(s)

        left = lax.rem(z + NZ - i, NZ)
        right = lax.rem(z + i + 1, NZ)
        after = jnp.minimum(i + 1, 3)
        scores_of(left, logit_a, i, git_a, right, logit_b, i, gpad_b, git_b)
        scores_of(
            right, logit_b, i, git_b, lax.rem(z + NZ - after, NZ), logit_a, after, gpad_a, git_a
        )
        return carry

    lax.fori_loop(0, NZ // 2, forward, 0)

    top = jnp.max(mx[...], axis=0, keepdims=True)
    total = sm[...] * jnp.exp2((mx[...] - top) * scale2)
    stat[me] = jnp.concatenate(
        [
            top,
            jnp.sum(total, axis=0, keepdims=True),
            jnp.sum(ps[...], axis=0, keepdims=True),
            jnp.zeros((5, US), F32),
        ],
        axis=0,
    )
    st_sends = [rc(stat.at[me], stat.at[me], st_s.at[i], st_r.at[i], quad[i]) for i in range(3)]
    for s in st_sends:
        s.start()
    for s in st_sends:
        s.wait_recv()
    st = [stat[i] for i in range(4)]
    all_top = jnp.maximum(jnp.maximum(st[0][0:1], st[1][0:1]), jnp.maximum(st[2][0:1], st[3][0:1]))
    inv_row = inv_t[0:1]
    all_sum = all_pos = None
    for i in range(4):
        part = st[i][1:2] * jnp.exp((st[i][0:1] - all_top) * inv_row)
        all_sum = part if all_sum is None else all_sum + part
        all_pos = st[i][2:3] if all_pos is None else all_pos + st[i][2:3]
    log_total = all_top * inv_row + jnp.log(all_sum)
    loss = log_total - all_pos * inv_row
    loss_ref[...] = jnp.where(jnp.broadcast_to(c, (1, UB)) == 0, loss[:, :UB], loss[:, UB:])
    ltb[...] = jnp.broadcast_to(log_total * LOG2E, (8, US))

    ones_row = lax.broadcasted_iota(jnp.int32, (8, 2 * CH), 0)
    ones_col = lax.broadcasted_iota(jnp.int32, (8, 2 * CH), 1) // CH
    ones = jnp.where(ones_row == ones_col, 1.0, 0.0).astype(BF16)

    def gate_copy(dr, d):
        far = 2 if d == 4 else 1
        return rc(
            gsend.at[dr, d - 1], grecv.at[dr, d - 1], g_s.at[dr, d - 1], g_r.at[dr, d - 1],
            dev(z + far * (2 * dr - 1), c, x),
        )

    def rs_copy(dr, d, h):
        far = 2 if d == 4 else 1
        return rc(
            sbuf.at[dr, d - 1, h], rbuf.at[dr, d - 1, h], rs_s.at[dr, d - 1, h], rs_r.at[dr, d - 1, h],
            dev(z + far * (2 * dr - 1), c, x),
        )

    def last_copy(dr, w):
        h = x if w == 0 else 1 - x
        return rc(
            sbuf.at[dr, 0, h], rbuf.at[dr, 0, w], rs_s.at[dr, 0, w], rs_r.at[dr, 0, w],
            dev(z + 2 * dr - 1, c, h),
        )

    def matmuls(o, lg, igp, r):
        both = jnp.dot(
            lg[pl.ds(pl.multiple_of(r * 2 * CH, 2 * CH), 2 * CH), :], qpair[r], preferred_element_type=F32
        )
        ib[r] = jnp.where(lane[:CH] < 64, both[:CH], both[CH:])
        for kk in range(2):
            at = pl.ds(pl.multiple_of(r * CH + kk * 64, 64), 64)
            part = jnp.dot(
                ctall[o, at, :],
                lg[pl.ds(pl.multiple_of((2 * r + kk) * CH, CH), CH), :],
                preferred_element_type=F32,
            )
            uacc[0, at, :] += part[:, :UB]
            uacc[1, at, :] += part[:, UB:]
        gates = igp[r]
        hi = gates.astype(BF16)
        lo = (gates - hi.astype(F32)).astype(BF16)
        gacc[r] = lax.dot_general(ones, hi, NT, preferred_element_type=F32) + lax.dot_general(
            ones, lo, NT, preferred_element_type=F32
        )

    def item_sum(h):
        return jnp.concatenate([ib[2 * h], ib[2 * h + 1]], axis=1)

    def gate_sum():
        return jnp.concatenate([gacc[i, 0:2, :] for i in range(4)], axis=0)

    def four(v):
        return jnp.concatenate([v] * (BROWS // 8), axis=0)

    def chunk(o, logit, s, lg, igp, o_before, lg_before, igp_before):
        def rows_of(r, carry):
            rows = pl.ds(pl.multiple_of(r * BROWS, BROWS), BROWS)
            matmuls(o_before, lg_before, igp_before, r)
            sc = score[o, rows, :]
            soft = jnp.exp2(sc * four(scale2) - four(ltb[...]))
            soft = jnp.where(is_positive(o, r, BROWS), soft - 1.0, soft) * four(inv_t)
            share = soft * dinv[o, rows, :]
            for k in range(K):
                l = logit[s, k, rows, :]
                t = jnp.tanh(l)
                g = weight[o, k, rows, :] * share
                gg = g * (l - sc)
                sk = slope_ref[k]
                out = g + gg * (sk - (t * t) * sk)
                lg[pl.ds(pl.multiple_of(k * CH + r * BROWS, BROWS), BROWS), :] = out.astype(BF16)
                ugv[k] = ugv[k] + ((gg[:8] + gg[8:16]) + (gg[16:24] + gg[24:]))
                igp[k // 2, rows, (k % 2) * CH : (k % 2 + 1) * CH] = (
                    gg[:, 0:128] + gg[:, 128:256]
                ) + (gg[:, 256:384] + gg[:, 384:512])
            return carry

        lax.fori_loop(0, CH // BROWS, rows_of, 0, unroll=True)

    def send(dr, jj):
        @pl.when(jj == 1)
        def _():
            for h in range(2):
                sbuf[dr, 2, h] = item_sum(h).astype(BF16)
                rs_copy(dr, 3, h).start()
            gsend[dr, 2] = gate_sum()
            gate_copy(dr, 3).start()

        @pl.when(jj == 2)
        def _():
            for h in range(2):
                rs_copy(dr, 3, h).wait_recv()
                value = item_sum(h) + rbuf[dr, 2, h].astype(F32)
                if h == dr:
                    rs_copy(dr, 4, h).wait_recv()
                    value = value + rbuf[dr, 3, h].astype(F32)
                sbuf[dr, 1, h] = value.astype(BF16)
                rs_copy(dr, 2, h).start()
            gate_copy(dr, 3).wait_recv()
            value = gate_sum() + grecv[dr, 2]
            if dr == 0:
                gate_copy(0, 4).wait_recv()
                value = value + grecv[0, 3]
            gsend[dr, 1] = value
            gate_copy(dr, 2).start()

        @pl.when(jj == 3)
        def _():
            for h in range(2):
                rs_copy(dr, 2, h).wait_recv()
                sbuf[dr, 0, h] = (item_sum(h) + rbuf[dr, 1, h].astype(F32)).astype(BF16)
            for w in (1, 0):
                last_copy(dr, w).start()
            gate_copy(dr, 2).wait_recv()
            gsend[dr, 0] = gate_sum() + grecv[dr, 1]
            gate_copy(dr, 1).start()

    def backward(jj, carry):
        d = 4 - jj
        right = lax.rem(z + d, NZ)
        chunk(right, logit_b, d - 1, lg_a, igp_a, lax.rem(z + NZ - d, NZ), lg_b, igp_b)
        send(0, jj)
        chunk(lax.rem(z + NZ - (d - 1), NZ), logit_a, d - 1, lg_b, igp_b, right, lg_a, igp_a)

        @pl.when(jj == 0)
        def _():
            for h in range(2):
                sbuf[h, 3, h] = item_sum(h).astype(BF16)
                rs_copy(h, 4, h).start()
            gsend[0, 3] = gate_sum()
            gate_copy(0, 4).start()

        send(1, jj)
        return carry

    lax.fori_loop(0, NZ // 2, backward, 0)

    for k in range(K):
        ugsend[k : k + 1, :] = jnp.sum(ugv[k], axis=0, keepdims=True)
    ug_sends = [rc(ugsend, ugrecv.at[i], ugs_s.at[i], ugs_r.at[i], quad[i]) for i in range(3)]
    for s in ug_sends:
        s.start()

    def u_core(hh, p):
        h = 1 - x if hh == 0 else x
        at = pl.ds(pl.multiple_of(h * UB + p * CH, CH), CH)
        return rc(uacc.at[1 - c, at, :], urecv.at[hh, p], uc_s.at[hh, p], uc_r.at[hh, p], cp)

    def u_x(p):
        return rc(usend.at[p], uxrecv.at[p], ux_s.at[p], ux_r.at[p], xp)

    def core_sum(hh, p):
        h = 1 - x if hh == 0 else x
        at = pl.ds(pl.multiple_of(h * UB + p * CH, CH), CH)
        u_core(hh, p).wait_recv()
        return uacc[c, at, :] + urecv[hh, p]

    for hh in range(2):
        for p in range(2):
            h = 1 - x if hh == 0 else x
            matmuls(z, lg_b, igp_b, 2 * h + p)
            u_core(hh, p).start()
    for p in range(2):
        usend[p] = core_sum(0, p).astype(BF16)
        u_x(p).start()

    sums = [item_sum(h) for h in range(2)]
    first = jnp.broadcast_to(x, (CH, UB)) == 0
    isend[...] = jnp.where(first, sums[1], sums[0]).astype(BF16)
    keep = jnp.where(first, sums[0], sums[1])
    i_x = rc(isend, irecv, fx_s.at[0], fx_r.at[0], xp)
    i_x.start()
    gate = gate_sum()
    for dr in range(2):
        gate_copy(dr, 1).wait_recv()
        gate = gate + grecv[dr, 0]
    igx[0] = gate
    ig_x = rc(igx.at[0], igx.at[1], fx_s.at[1], fx_r.at[1], xp)
    ig_x.start()

    for p in range(2):
        ukeep[p * CH : (p + 1) * CH, :] = core_sum(1, p)
    for s in ug_sends:
        s.wait_recv()
    ugate = (ugsend[...] + ugrecv[0]) + (ugrecv[1] + ugrecv[2])
    ugate = jnp.where(jnp.broadcast_to(c, (K, UB)) == 0, ugate[:, :UB], ugate[:, UB:])
    ugate_ref[...] = jnp.where(jnp.broadcast_to(x, (4, UB)) == 0, ugate[:4], ugate[4:])

    for dr in range(2):
        last_copy(dr, 0).wait_recv()
    ig_ref[own_rows, :] = keep + (rbuf[0, 0, 0].astype(F32) + rbuf[1, 0, 0].astype(F32))
    for dr in range(2):
        last_copy(dr, 1).wait_recv()
    i_x.wait_recv()
    ig_ref[peer_rows, :] = irecv[...].astype(F32) + (
        rbuf[0, 0, 1].astype(F32) + rbuf[1, 0, 1].astype(F32)
    )
    ig_x.wait_recv()
    mine, theirs = igx[0], igx[1]
    upper = jnp.concatenate([mine, theirs], axis=1)[:4]
    lower = jnp.concatenate([theirs, mine], axis=1)[4:]
    igate_ref[...] = jnp.where(jnp.broadcast_to(x, (4, UB)) == 0, upper, lower)
    for p in range(2):
        u_x(p).wait_recv()
        at = slice(p * CH, (p + 1) * CH)
        ug_ref[:, at] = (ukeep[at, :] + uxrecv[p].astype(F32)).T

    for s in (x_item, q_x, q_c, q_f, *u_sends, *st_sends, i_x, ig_x, *ug_sends):
        s.wait_send()
    for p in range(2):
        u_x(p).wait_send()
        for hh in range(2):
            u_core(hh, p).wait_send()
    gate_copy(0, 4).wait_send()
    for dr in range(2):
        rs_copy(dr, 4, dr).wait_send()
        for d in (1, 2, 3):
            gate_copy(dr, d).wait_send()
        for w in range(2):
            last_copy(dr, w).wait_send()
            for d in (2, 3):
                rs_copy(dr, d, w).wait_send()
        for hh in range(2):
            for s in range(1, 5 if hh == dr else 4):
                for n in range(2):
                    hop(dr, s, hh, n).wait_send()


def write_out(loss, ug, ig, ugate, igate, *outs):
    for a, o in zip((loss, ug, ig, ugate, igate), outs):
        o[...] = a[...]


def body(query, candidate, query_gate, candidate_gate, slope, scale, target):
    vmem = pl.BlockSpec(memory_space=pltpu.VMEM)
    smem = pl.BlockSpec(memory_space=pltpu.SMEM)
    dma = pltpu.SemaphoreType.DMA
    scratch = [
        pltpu.VMEM((2, 2, UB, UB), BF16),
        pltpu.VMEM((4, 8, UB), F32),
        pltpu.VMEM((NZ, 2, SLOT, UB), BF16),
        pltpu.VMEM((SLOT, UB), BF16),
        pltpu.VMEM((CH, CH), F32),
        pltpu.VMEM((CH, CH), F32),
        pltpu.VMEM((CH, CH), F32),
        pltpu.VMEM((CH, CH), F32),
        pltpu.VMEM((NZ, K * 64, CH), BF16),
        pltpu.VMEM((K, US, CH), BF16),
        pltpu.VMEM((K, 8, US), F32),
        pltpu.VMEM((8, US), F32),
        pltpu.VMEM((NZ // 2, K, CH, US), F32),
        pltpu.VMEM((NZ // 2, K, CH, US), F32),
        pltpu.VMEM((NZ, K, CH, US), F32),
        pltpu.VMEM((NZ, CH, US), F32),
        pltpu.VMEM((NZ, CH, US), F32),
        pltpu.VMEM((8, US), F32),
        pltpu.VMEM((8, US), F32),
        pltpu.VMEM((8, US), F32),
        pltpu.VMEM((4, 8, US), F32),
        pltpu.VMEM((8, US), F32),
        pltpu.VMEM((K * CH, US), BF16),
        pltpu.VMEM((K * CH, US), BF16),
        pltpu.VMEM((4, CH, 2 * CH), F32),
        pltpu.VMEM((4, CH, 2 * CH), F32),
        pltpu.VMEM((4, 8, CH), F32),
        pltpu.VMEM((K, 8, US), F32),
        pltpu.VMEM((2, US, UB), F32),
        pltpu.VMEM((4, CH, CH), F32),
        pltpu.VMEM((4, US, CH), BF16),
        pltpu.VMEM((2, 4, 2, CH, UB), BF16),
        pltpu.VMEM((2, 4, 2, CH, UB), BF16),
        pltpu.VMEM((2, 4, K, CH), F32),
        pltpu.VMEM((2, 4, K, CH), F32),
        pltpu.VMEM((2, 2, CH, UB), F32),
        pltpu.VMEM((UB, UB), F32),
        pltpu.VMEM((2, CH, UB), BF16),
        pltpu.VMEM((2, CH, UB), BF16),
        pltpu.VMEM((CH, UB), BF16),
        pltpu.VMEM((CH, UB), BF16),
        pltpu.VMEM((2, K, CH), F32),
        pltpu.VMEM((K, US), F32),
        pltpu.VMEM((3, K, US), F32),
        dma((1,)), dma((1,)),
        dma((3,)), dma((3,)),
        dma((3,)), dma((3,)),
        dma((2, 4, 2, 2)), dma((2, 4, 2, 2)),
        dma((3,)), dma((3,)),
        dma((2, 4, 2)), dma((2, 4, 2)),
        dma((2, 4)), dma((2, 4)),
        dma((2, 2)), dma((2, 2)),
        dma((2,)), dma((2,)),
        dma((2,)), dma((2,)),
        dma((3,)), dma((3,)),
    ]
    outs = (
        jax.ShapeDtypeStruct((1, UB), F32),
        jax.ShapeDtypeStruct((UB, UB), F32),
        jax.ShapeDtypeStruct((UB, UB), F32),
        jax.ShapeDtypeStruct((4, UB), F32),
        jax.ShapeDtypeStruct((4, UB), F32),
    )
    results = pl.pallas_call(
        kernel,
        out_shape=outs,
        in_specs=[vmem, vmem, vmem, vmem, smem, smem, vmem],
        out_specs=(vmem,) * 5,
        scratch_shapes=scratch,
        compiler_params=pltpu.CompilerParams(
            collective_id=0, has_side_effects=True, vmem_limit_bytes=60 * 1024 * 1024
        ),
    )(query, candidate, query_gate, candidate_gate, slope, scale, target.reshape(1, UB))
    loss, ug, ig, ugate, igate = pl.pallas_call(
        write_out, out_shape=outs, in_specs=[vmem] * 5, out_specs=(vmem,) * 5
    )(*results)
    return loss.reshape(UB), ug, ig, ugate, igate


def solution(mesh):
    in_specs = (
        P(("task", "blk"), "comp"),
        P(("task", "blk"), "comp"),
        P("comp", ("task", "blk")),
        P("comp", ("task", "blk")),
        P(),
        P("task"),
        P(("task", "blk")),
    )
    out_specs = (
        P(("task", "blk")),
        P(("task", "blk"), "comp"),
        P(("task", "blk"), "comp"),
        P("comp", ("task", "blk")),
        P("comp", ("task", "blk")),
    )
    return jax.shard_map(body, mesh=mesh, in_specs=in_specs, out_specs=out_specs, check_vma=False)
```

```python
import jax
import jax.numpy as jnp
from jax import lax
from jax.experimental import pallas as pl
from jax.experimental.pallas import tpu as pltpu
from jax.sharding import PartitionSpec as P

MESH = pl.DeviceIdType.MESH
LOG2E = 1.4426950408889634
F32, BF16 = jnp.float32, jnp.bfloat16
NZ = 8
UB = 256
US = 512
CH = 128
SLOT = CH + 16
PIECES = ((0, 80), (80, 64))
K = 8
ROWS = 16
BROWS = 32
NT = (((1,), (1,)), ((), ()))


def kernel(
    q_ref, c_ref, gq_ref, gc_ref, slope_ref, t_ref, tgt_ref,
    loss_ref, ug_ref, ig_ref, ugate_ref, igate_ref,
    qall, ugall, call, xstage, gpad_a, gpad_b, git_a, git_b, ctall, qm, gub, tgtb,
    logit_a, logit_b, weight, score, dinv, mx, sm, ps, stat, ltb,
    lg_a, lg_b, igp_a, igp_b, gacc_a, gacc_b, gacc_c, ugv, uacc, ib_a, ib_b, ib_c, qpair, sbuf, rbuf, gsend, grecv,
    urecv, ukeep, usend, uxrecv, isend, irecv, keep, igx, ugsend, ugrecv,
    x_s, x_r, q_s, q_r, u_s, u_r, ag_s, ag_r, st_s, st_r,
    rs_s, rs_r, g_s, g_r, uc_s, uc_r, ux_s, ux_r, fx_s, fx_r, ugs_s, ugs_r,
):
    blk = lax.axis_index("blk")
    x = lax.axis_index("comp")
    z = blk // 2
    c = lax.rem(blk, 2)
    me = 2 * x + c

    def dev(zz, cc, xx):
        return {"blk": lax.rem(zz + NZ, NZ) * 2 + cc, "comp": xx}

    def rc(src, dst, ss, rs, device):
        return pltpu.make_async_remote_copy(
            src_ref=src, dst_ref=dst, send_sem=ss, recv_sem=rs, device_id=device, device_id_type=MESH
        )

    xp, cp, dp = dev(z, c, 1 - x), dev(z, 1 - c, x), dev(z, 1 - c, 1 - x)
    quad = (xp, cp, dp)

    barrier = pltpu.get_barrier_semaphore()
    near = [dev(z + d, c, x) for d in (-2, -1, 1, 2, 4)] + [dev(z + d, c, 1 - x) for d in (-1, 1, 4)]
    for peer in (*quad, *near):
        pl.semaphore_signal(barrier, inc=1, device_id=peer, device_id_type=MESH)

    own_rows = pl.ds(pl.multiple_of(x * CH, CH), CH)
    peer_rows = pl.ds(pl.multiple_of((1 - x) * CH, CH), CH)
    gc = gc_ref[...].astype(F32)
    gc = jnp.concatenate([gc, gc], axis=0)
    gc = jnp.concatenate([gc, gc], axis=0)
    low = jnp.broadcast_to(x, (16, CH)) == 0
    blank = jnp.zeros((16, CH), F32)
    own_gate = jnp.concatenate([jnp.where(low, gc[:, :CH], gc[:, CH:]), blank], axis=1)
    peer_gate = jnp.concatenate([jnp.where(low, gc[:, CH:], gc[:, :CH]), blank], axis=1)
    call[z, x, :CH, :] = c_ref[own_rows, :]
    call[z, x, CH:, :] = own_gate.astype(BF16)
    xstage[:CH, :] = c_ref[peer_rows, :]
    xstage[CH:, :] = peer_gate.astype(BF16)
    qall[c, x] = q_ref[...]
    gq = gq_ref[...].astype(F32)
    ugall[me] = jnp.concatenate([gq, jnp.broadcast_to(tgt_ref[...].astype(F32), (4, UB))], axis=0)

    pl.semaphore_wait(barrier, len(quad) + len(near))

    def hop(dr, s, hh, n):
        step = 1 - 2 * dr
        o = lax.rem(z - step * min(s - 1, 2) + NZ, NZ)
        h = x if hh == 0 else 1 - x
        at = call.at[o, h, pl.ds(*PIECES[n]), :]
        return rc(at, at, ag_s.at[dr, s - 1, hh, n], ag_r.at[dr, s - 1, hh, n],
                  dev(z + (2 * step if s == 4 else step), c, x))

    def arrive(s, halves=(0, 1)):
        for hh in halves:
            for n in range(2):
                for dr in range(2):
                    if s < 4 or hh == dr:
                        hop(dr, s, hh, n).wait_recv()
                    if s == 2 and hh == dr:
                        hop(dr, 4, hh, n).start()
                    if s < 3:
                        hop(dr, s + 1, hh, n).start()

    x_item = rc(xstage, call.at[z, x], x_s.at[0], x_r.at[0], xp)
    q_x = rc(q_ref, qall.at[c, x], q_s.at[0], q_r.at[0], xp)
    q_c = rc(q_ref, qall.at[c, x], q_s.at[1], q_r.at[1], cp)
    q_f = rc(qall.at[c, 1 - x], qall.at[c, 1 - x], q_s.at[2], q_r.at[2], cp)
    u_sends = [rc(ugall.at[me], ugall.at[me], u_s.at[i], u_r.at[i], quad[i]) for i in range(3)]
    x_item.start()
    for n in range(2):
        hop(0, 1, 0, n).start()
        hop(1, 1, 0, n).start()
    q_x.start()
    for s in u_sends:
        s.start()
    q_c.start()

    gpad_a[...] = jnp.zeros_like(gpad_a)
    gpad_b[...] = jnp.zeros_like(gpad_b)
    mx[...] = jnp.full(mx.shape, -3.0e38, F32)
    sm[...] = jnp.zeros_like(sm)
    ps[...] = jnp.zeros_like(ps)
    uacc[...] = jnp.zeros_like(uacc)
    ugv[...] = jnp.zeros_like(ugv)
    lg_b[...] = jnp.zeros_like(lg_b)
    igp_b[...] = jnp.zeros_like(igp_b)

    x_item.wait_recv()
    for n in range(2):
        hop(0, 1, 1, n).start()
        hop(1, 1, 1, n).start()
    q_x.wait_recv()
    q_f.start()
    arrive(1, (0,))

    lane = lax.broadcasted_iota(jnp.int32, (UB, CH), 1)

    def mask_users(cc, h):
        for p in range(2):
            rows = pl.ds(pl.multiple_of(cc * UB, UB), UB)
            k = 4 * h + 2 * p
            qpair[k // 2, rows, :] = qall[cc, h, :, p * CH : (p + 1) * CH]
            pair = qall[cc, h, :, p * CH : (p + 1) * CH].astype(F32)
            qm[k, rows, :] = jnp.where(lane < 64, pair, 0.0).astype(BF16)
            qm[k + 1, rows, :] = jnp.where(lane < 64, 0.0, pair).astype(BF16)

    for h in range(2):
        mask_users(c, h)
    for s in u_sends:
        s.wait_recv()
    for k in range(K):
        h, r = k // 4, k % 4
        row = jnp.concatenate([ugall[2 * h, r : r + 1, :], ugall[2 * h + 1, r : r + 1, :]], axis=1)
        gub[k] = jnp.broadcast_to(row * LOG2E, (8, US))
    tgtb[...] = jnp.broadcast_to(
        jnp.concatenate([ugall[0, 4:5, :], ugall[1, 4:5, :]], axis=1), (8, US)
    )
    q_c.wait_recv()
    q_f.wait_recv()
    for h in range(2):
        mask_users(1 - c, h)

    inv_t = 1.0 / jnp.full((8, US), t_ref[0], F32)
    scale2 = inv_t * LOG2E

    def twice(v):
        return jnp.concatenate([v, v], axis=0)

    def is_positive(o, r, rows):
        ids = lax.broadcasted_iota(jnp.int32, (rows, US), 0) + (
            (o * 2 + c) * UB + x * CH + r * rows
        )
        return jnp.concatenate([tgtb[...]] * (rows // 8), axis=0) == ids.astype(F32)

    def gates_of(o, gpad, git):
        gpad[0:16, :] = call[o, 0, CH:, :CH].astype(F32)
        gpad[16:32, :] = call[o, 1, CH:, :CH].astype(F32)
        git[...] = gpad[...].T * LOG2E

    def logits_of(o, logit, s, k):
        h, p = k // 4, lax.rem(k, 4) // 2
        at = pl.ds(pl.multiple_of(p * CH, CH), CH)
        logit[s, k] = lax.dot_general(call[o, h, :CH, at], qm[k], NT, preferred_element_type=F32)

    def scores_of(o, logit, s, git, o_next, logit_next, s_next, gpad_next, git_next):
        gates_of(o_next, gpad_next, git_next)
        for h in range(2):
            for p in range(2):
                at = slice((2 * h + p) * CH, (2 * h + p + 1) * CH)
                ctall[o, at, :] = call[o, h, :CH, p * CH : (p + 1) * CH].T

        def rows_of(r, carry):
            top, pos = carry
            logits_of(o_next, logit_next, s_next, r)
            rows = pl.ds(pl.multiple_of(r * ROWS, ROWS), ROWS)
            den = num = None
            gcols = git[rows, :]
            for k in range(K):
                col = (k // 4) * 16 + k % 4
                l = logit[s, k, rows, :]
                e = jnp.tanh(l) * (slope_ref[k] * LOG2E) + gcols[:, col : col + 1] + twice(gub[k])
                w = jnp.exp2(e)
                weight[o, k, rows, :] = w
                wl = w * l
                den = w if den is None else den + w
                num = wl if num is None else num + wl
            di = 1.0 / den
            sc = num * di
            dinv[o, rows, :] = di
            score[o, rows, :] = sc
            hit = jnp.where(is_positive(o, r, ROWS), sc, 0.0)
            return (
                jnp.maximum(top, jnp.maximum(sc[:8], sc[8:])),
                pos + hit[:8] + hit[8:],
            )

        before = mx[...]
        top, pos = lax.fori_loop(0, CH // ROWS, rows_of, (before, ps[...]), unroll=True)
        mx[...] = top
        ps[...] = pos
        shift = top * scale2
        total = sm[...] * jnp.exp2((before - top) * scale2)
        for m in range(CH // 8):
            total = total + jnp.exp2(score[o, m * 8 : (m + 1) * 8, :] * scale2 - shift)
        sm[...] = total

    arrive(1, (1,))
    gates_of(z, gpad_a, git_a)

    def own_logits(k, carry):
        logits_of(z, logit_a, 0, k)
        return carry

    lax.fori_loop(0, K, own_logits, 0, unroll=True)

    def forward(i, carry):
        for s in (2, 3, 4):

            @pl.when(i == s - 1)
            def _():
                arrive(s)

        left = lax.rem(z + NZ - i, NZ)
        right = lax.rem(z + i + 1, NZ)
        after = jnp.minimum(i + 1, 3)
        scores_of(left, logit_a, i, git_a, right, logit_b, i, gpad_b, git_b)
        scores_of(
            right, logit_b, i, git_b, lax.rem(z + NZ - after, NZ), logit_a, after, gpad_a, git_a
        )
        return carry

    lax.fori_loop(0, NZ // 2, forward, 0)

    top = jnp.max(mx[...], axis=0, keepdims=True)
    total = sm[...] * jnp.exp2((mx[...] - top) * scale2)
    stat[me] = jnp.concatenate(
        [
            top,
            jnp.sum(total, axis=0, keepdims=True),
            jnp.sum(ps[...], axis=0, keepdims=True),
            jnp.zeros((5, US), F32),
        ],
        axis=0,
    )
    st_sends = [rc(stat.at[me], stat.at[me], st_s.at[i], st_r.at[i], quad[i]) for i in range(3)]
    for s in st_sends:
        s.start()
    for s in st_sends:
        s.wait_recv()
    st = [stat[i] for i in range(4)]
    all_top = jnp.maximum(jnp.maximum(st[0][0:1], st[1][0:1]), jnp.maximum(st[2][0:1], st[3][0:1]))
    inv_row = inv_t[0:1]
    all_sum = all_pos = None
    for i in range(4):
        part = st[i][1:2] * jnp.exp((st[i][0:1] - all_top) * inv_row)
        all_sum = part if all_sum is None else all_sum + part
        all_pos = st[i][2:3] if all_pos is None else all_pos + st[i][2:3]
    log_total = all_top * inv_row + jnp.log(all_sum)
    loss = log_total - all_pos * inv_row
    loss_ref[...] = jnp.where(jnp.broadcast_to(c, (1, UB)) == 0, loss[:, :UB], loss[:, UB:])
    ltb[...] = jnp.broadcast_to(log_total * LOG2E, (8, US))

    ones_row = lax.broadcasted_iota(jnp.int32, (8, 2 * CH), 0)
    ones_col = lax.broadcasted_iota(jnp.int32, (8, 2 * CH), 1) // CH
    ones = jnp.where(ones_row == ones_col, 1.0, 0.0).astype(BF16)

    def gate_copy(dr, d):
        far = 4 if d == 4 else 1
        return rc(
            gsend.at[dr, d - 1], grecv.at[dr, d - 1], g_s.at[dr, d - 1], g_r.at[dr, d - 1],
            dev(z + far * (2 * dr - 1), c, x),
        )

    def rs_copy(dr, d, h):
        far = 4 if d == 4 else 1
        return rc(
            sbuf.at[dr, d - 1, h], rbuf.at[dr, d - 1, h], rs_s.at[dr, d - 1, h], rs_r.at[dr, d - 1, h],
            dev(z + far * (2 * dr - 1), c, x),
        )

    def far_copy(w):
        h = x if w == 0 else 1 - x
        return rc(
            sbuf.at[0, 3, h], rbuf.at[0, 3, w], rs_s.at[0, 3, w], rs_r.at[0, 3, w], dev(z + 4, c, h)
        )

    def last_copy(dr, w):
        h = x if w == 0 else 1 - x
        return rc(
            sbuf.at[dr, 0, h], rbuf.at[dr, 0, w], rs_s.at[dr, 0, w], rs_r.at[dr, 0, w],
            dev(z + 2 * dr - 1, c, h),
        )

    def matmuls(o, lg, igp, ib, gacc, r):
        both = jnp.dot(
            lg[pl.ds(pl.multiple_of(r * 2 * CH, 2 * CH), 2 * CH), :], qpair[r], preferred_element_type=F32
        )
        ib[r] = jnp.where(lane[:CH] < 64, both[:CH], both[CH:])
        for kk in range(2):
            at = pl.ds(pl.multiple_of(r * CH + kk * 64, 64), 64)
            part = jnp.dot(
                ctall[o, at, :],
                lg[pl.ds(pl.multiple_of((2 * r + kk) * CH, CH), CH), :],
                preferred_element_type=F32,
            )
            uacc[0, at, :] += part[:, :UB]
            uacc[1, at, :] += part[:, UB:]
        gates = igp[r]
        hi = gates.astype(BF16)
        lo = (gates - hi.astype(F32)).astype(BF16)
        gacc[r] = lax.dot_general(ones, hi, NT, preferred_element_type=F32) + lax.dot_general(
            ones, lo, NT, preferred_element_type=F32
        )

    def item_sum(ib, h):
        return jnp.concatenate([ib[2 * h], ib[2 * h + 1]], axis=1)

    def gate_sum(gacc):
        return jnp.concatenate([gacc[i, 0:2, :] for i in range(4)], axis=0)

    def four(v):
        return jnp.concatenate([v] * (BROWS // 8), axis=0)

    def chunk(o, logit, s, lg, igp, o_before, lg_before, igp_before, ib, gacc):
        def rows_of(r, carry):
            rows = pl.ds(pl.multiple_of(r * BROWS, BROWS), BROWS)
            matmuls(o_before, lg_before, igp_before, ib, gacc, r)
            sc = score[o, rows, :]
            soft = jnp.exp2(sc * four(scale2) - four(ltb[...]))
            soft = jnp.where(is_positive(o, r, BROWS), soft - 1.0, soft) * four(inv_t)
            share = soft * dinv[o, rows, :]
            for k in range(K):
                l = logit[s, k, rows, :]
                t = jnp.tanh(l)
                g = weight[o, k, rows, :] * share
                gg = g * (l - sc)
                sk = slope_ref[k]
                out = g + gg * (sk - (t * t) * sk)
                lg[pl.ds(pl.multiple_of(k * CH + r * BROWS, BROWS), BROWS), :] = out.astype(BF16)
                ugv[k] = ugv[k] + ((gg[:8] + gg[8:16]) + (gg[16:24] + gg[24:]))
                igp[k // 2, rows, (k % 2) * CH : (k % 2 + 1) * CH] = (
                    gg[:, 0:128] + gg[:, 128:256]
                ) + (gg[:, 256:384] + gg[:, 384:512])
            return carry

        lax.fori_loop(0, CH // BROWS, rows_of, 0, unroll=True)

    def send(dr, d, ib, gacc):
        if d == 3:
            for h in range(2):
                sbuf[dr, 2, h] = item_sum(ib, h).astype(BF16)
                rs_copy(dr, 3, h).start()
            gsend[dr, 2] = gate_sum(gacc)
            gate_copy(dr, 3).start()
        elif d == 2:
            for h in range(2):
                rs_copy(dr, 3, h).wait_recv()
                value = item_sum(ib, h) + rbuf[dr, 2, h].astype(F32)
                sbuf[dr, 1, h] = value.astype(BF16)
                rs_copy(dr, 2, h).start()
            gate_copy(dr, 3).wait_recv()
            gsend[dr, 1] = gate_sum(gacc) + grecv[dr, 2]
            gate_copy(dr, 2).start()
        else:
            for h in range(2):
                rs_copy(dr, 2, h).wait_recv()
                sbuf[dr, 0, h] = (item_sum(ib, h) + rbuf[dr, 1, h].astype(F32)).astype(BF16)
            for w in (1, 0):
                last_copy(dr, w).start()
            gate_copy(dr, 2).wait_recv()
            gsend[dr, 0] = gate_sum(gacc) + grecv[dr, 1]
            gate_copy(dr, 1).start()

    first = jnp.broadcast_to(x, (CH, UB)) == 0
    i_x = rc(isend, irecv, fx_s.at[0], fx_r.at[0], xp)

    def backward(jj, carry):
        a = jnp.where(jj == 0, 3, jnp.where(jj == 1, 0, 4 - jj))
        b = jnp.where(jj == 2, 3, jnp.where(jj == 3, 0, 2 - jj))
        b_before = jnp.where(jj == 3, 3, 3 - jj)
        left = lax.rem(z + NZ - a, NZ)
        right = lax.rem(z + b + 1, NZ)
        right_before = lax.rem(z + lax.rem(b_before, 4) + 1, NZ)
        chunk(left, logit_a, a, lg_a, igp_a, right_before, lg_b, igp_b, ib_a, gacc_a)

        @pl.when(jj == 1)
        def _():
            send(1, 3, ib_a, gacc_a)

        @pl.when(jj == 3)
        def _():
            for h in range(2):
                sbuf[0, 3, h] = item_sum(ib_a, h).astype(BF16)
            for w in range(2):
                far_copy(w).start()
            gsend[0, 3] = gate_sum(gacc_a)
            gate_copy(0, 4).start()

        chunk(right, logit_b, b, lg_b, igp_b, left, lg_a, igp_a, ib_b, gacc_b)

        @pl.when(jj == 0)
        def _():
            send(0, 3, ib_b, gacc_b)

        @pl.when(jj == 1)
        def _():
            sums = [item_sum(ib_b, h) for h in range(2)]
            isend[...] = jnp.where(first, sums[1], sums[0]).astype(BF16)
            keep[...] = jnp.where(first, sums[0], sums[1])
            i_x.start()
            igx[0] = gate_sum(gacc_b)

        @pl.when(jj == 2)
        def _():
            send(0, 2, ib_b, gacc_b)
            send(1, 2, ib_a, gacc_a)

        return carry

    lax.fori_loop(0, NZ // 2, backward, 0)

    def u_core(hh, p):
        h = 1 - x if hh == 0 else x
        at = pl.ds(pl.multiple_of(h * UB + p * CH, CH), CH)
        return rc(uacc.at[1 - c, at, :], urecv.at[hh, p], uc_s.at[hh, p], uc_r.at[hh, p], cp)

    def u_x(p):
        return rc(usend.at[p], uxrecv.at[p], ux_s.at[p], ux_r.at[p], xp)

    def core_sum(hh, p):
        h = 1 - x if hh == 0 else x
        at = pl.ds(pl.multiple_of(h * UB + p * CH, CH), CH)
        u_core(hh, p).wait_recv()
        return uacc[c, at, :] + urecv[hh, p]

    for hh in range(2):
        for p in range(2):
            h = 1 - x if hh == 0 else x
            matmuls(lax.rem(z + 1, NZ), lg_b, igp_b, ib_c, gacc_c, 2 * h + p)
            u_core(hh, p).start()
    send(0, 1, ib_b, gacc_b)
    send(1, 1, ib_c, gacc_c)
    for p in range(2):
        usend[p] = core_sum(0, p).astype(BF16)
        u_x(p).start()

    for k in range(K):
        ugsend[k : k + 1, :] = jnp.sum(ugv[k], axis=0, keepdims=True)
    ug_sends = [rc(ugsend, ugrecv.at[i], ugs_s.at[i], ugs_r.at[i], quad[i]) for i in range(3)]
    for s in ug_sends:
        s.start()
    gate_copy(0, 4).wait_recv()
    gate = igx[0] + grecv[0, 3]
    for dr in range(2):
        gate_copy(dr, 1).wait_recv()
        gate = gate + grecv[dr, 0]
    igx[0] = gate
    ig_x = rc(igx.at[0], igx.at[1], fx_s.at[1], fx_r.at[1], xp)
    ig_x.start()

    for p in range(2):
        ukeep[p * CH : (p + 1) * CH, :] = core_sum(1, p)
    for s in ug_sends:
        s.wait_recv()
    ugate = (ugsend[...] + ugrecv[0]) + (ugrecv[1] + ugrecv[2])
    ugate = jnp.where(jnp.broadcast_to(c, (K, UB)) == 0, ugate[:, :UB], ugate[:, UB:])
    ugate_ref[...] = jnp.where(jnp.broadcast_to(x, (4, UB)) == 0, ugate[:4], ugate[4:])

    for w in range(2):
        far_copy(w).wait_recv()
    for dr in range(2):
        last_copy(dr, 0).wait_recv()
    ig_ref[own_rows, :] = (keep[...] + rbuf[0, 3, 0].astype(F32)) + (
        rbuf[0, 0, 0].astype(F32) + rbuf[1, 0, 0].astype(F32)
    )
    for dr in range(2):
        last_copy(dr, 1).wait_recv()
    i_x.wait_recv()
    ig_ref[peer_rows, :] = (irecv[...].astype(F32) + rbuf[0, 3, 1].astype(F32)) + (
        rbuf[0, 0, 1].astype(F32) + rbuf[1, 0, 1].astype(F32)
    )
    ig_x.wait_recv()
    mine, theirs = igx[0], igx[1]
    upper = jnp.concatenate([mine, theirs], axis=1)[:4]
    lower = jnp.concatenate([theirs, mine], axis=1)[4:]
    igate_ref[...] = jnp.where(jnp.broadcast_to(x, (4, UB)) == 0, upper, lower)
    for p in range(2):
        u_x(p).wait_recv()
        at = slice(p * CH, (p + 1) * CH)
        ug_ref[:, at] = (ukeep[at, :] + uxrecv[p].astype(F32)).T

    for s in (x_item, q_x, q_c, q_f, *u_sends, *st_sends, i_x, ig_x, *ug_sends):
        s.wait_send()
    for p in range(2):
        u_x(p).wait_send()
        for hh in range(2):
            u_core(hh, p).wait_send()
    gate_copy(0, 4).wait_send()
    for dr in range(2):
        far_copy(dr).wait_send()
        for d in (1, 2, 3):
            gate_copy(dr, d).wait_send()
        for w in range(2):
            last_copy(dr, w).wait_send()
            for d in (2, 3):
                rs_copy(dr, d, w).wait_send()
        for hh in range(2):
            for s in range(1, 5 if hh == dr else 4):
                for n in range(2):
                    hop(dr, s, hh, n).wait_send()


def write_out(loss, ug, ig, ugate, igate, *outs):
    for a, o in zip((loss, ug, ig, ugate, igate), outs):
        o[...] = a[...]


def body(query, candidate, query_gate, candidate_gate, slope, scale, target):
    vmem = pl.BlockSpec(memory_space=pltpu.VMEM)
    smem = pl.BlockSpec(memory_space=pltpu.SMEM)
    dma = pltpu.SemaphoreType.DMA
    scratch = [
        pltpu.VMEM((2, 2, UB, UB), BF16),
        pltpu.VMEM((4, 8, UB), F32),
        pltpu.VMEM((NZ, 2, SLOT, UB), BF16),
        pltpu.VMEM((SLOT, UB), BF16),
        pltpu.VMEM((CH, CH), F32),
        pltpu.VMEM((CH, CH), F32),
        pltpu.VMEM((CH, CH), F32),
        pltpu.VMEM((CH, CH), F32),
        pltpu.VMEM((NZ, K * 64, CH), BF16),
        pltpu.VMEM((K, US, CH), BF16),
        pltpu.VMEM((K, 8, US), F32),
        pltpu.VMEM((8, US), F32),
        pltpu.VMEM((NZ // 2, K, CH, US), F32),
        pltpu.VMEM((NZ // 2, K, CH, US), F32),
        pltpu.VMEM((NZ, K, CH, US), F32),
        pltpu.VMEM((NZ, CH, US), F32),
        pltpu.VMEM((NZ, CH, US), F32),
        pltpu.VMEM((8, US), F32),
        pltpu.VMEM((8, US), F32),
        pltpu.VMEM((8, US), F32),
        pltpu.VMEM((4, 8, US), F32),
        pltpu.VMEM((8, US), F32),
        pltpu.VMEM((K * CH, US), BF16),
        pltpu.VMEM((K * CH, US), BF16),
        pltpu.VMEM((4, CH, 2 * CH), F32),
        pltpu.VMEM((4, CH, 2 * CH), F32),
        pltpu.VMEM((4, 8, CH), F32),
        pltpu.VMEM((4, 8, CH), F32),
        pltpu.VMEM((4, 8, CH), F32),
        pltpu.VMEM((K, 8, US), F32),
        pltpu.VMEM((2, US, UB), F32),
        pltpu.VMEM((4, CH, CH), F32),
        pltpu.VMEM((4, CH, CH), F32),
        pltpu.VMEM((4, CH, CH), F32),
        pltpu.VMEM((4, US, CH), BF16),
        pltpu.VMEM((2, 4, 2, CH, UB), BF16),
        pltpu.VMEM((2, 4, 2, CH, UB), BF16),
        pltpu.VMEM((2, 4, K, CH), F32),
        pltpu.VMEM((2, 4, K, CH), F32),
        pltpu.VMEM((2, 2, CH, UB), F32),
        pltpu.VMEM((UB, UB), F32),
        pltpu.VMEM((2, CH, UB), BF16),
        pltpu.VMEM((2, CH, UB), BF16),
        pltpu.VMEM((CH, UB), BF16),
        pltpu.VMEM((CH, UB), BF16),
        pltpu.VMEM((CH, UB), F32),
        pltpu.VMEM((2, K, CH), F32),
        pltpu.VMEM((K, US), F32),
        pltpu.VMEM((3, K, US), F32),
        dma((1,)), dma((1,)),
        dma((3,)), dma((3,)),
        dma((3,)), dma((3,)),
        dma((2, 4, 2, 2)), dma((2, 4, 2, 2)),
        dma((3,)), dma((3,)),
        dma((2, 4, 2)), dma((2, 4, 2)),
        dma((2, 4)), dma((2, 4)),
        dma((2, 2)), dma((2, 2)),
        dma((2,)), dma((2,)),
        dma((2,)), dma((2,)),
        dma((3,)), dma((3,)),
    ]
    outs = (
        jax.ShapeDtypeStruct((1, UB), F32),
        jax.ShapeDtypeStruct((UB, UB), F32),
        jax.ShapeDtypeStruct((UB, UB), F32),
        jax.ShapeDtypeStruct((4, UB), F32),
        jax.ShapeDtypeStruct((4, UB), F32),
    )
    results = pl.pallas_call(
        kernel,
        out_shape=outs,
        in_specs=[vmem, vmem, vmem, vmem, smem, smem, vmem],
        out_specs=(vmem,) * 5,
        scratch_shapes=scratch,
        compiler_params=pltpu.CompilerParams(
            collective_id=0, has_side_effects=True, vmem_limit_bytes=60 * 1024 * 1024
        ),
    )(query, candidate, query_gate, candidate_gate, slope, scale, target.reshape(1, UB))
    loss, ug, ig, ugate, igate = pl.pallas_call(
        write_out, out_shape=outs, in_specs=[vmem] * 5, out_specs=(vmem,) * 5
    )(*results)
    return loss.reshape(UB), ug, ig, ugate, igate


def solution(mesh):
    in_specs = (
        P(("task", "blk"), "comp"),
        P(("task", "blk"), "comp"),
        P("comp", ("task", "blk")),
        P("comp", ("task", "blk")),
        P(),
        P("task"),
        P(("task", "blk")),
    )
    out_specs = (
        P(("task", "blk")),
        P(("task", "blk"), "comp"),
        P(("task", "blk"), "comp"),
        P("comp", ("task", "blk")),
        P("comp", ("task", "blk")),
    )
    return jax.shard_map(body, mesh=mesh, in_specs=in_specs, out_specs=out_specs, check_vma=False)
```

```python
import jax
import jax.numpy as jnp
from jax import lax
from jax.experimental import pallas as pl
from jax.experimental.pallas import tpu as pltpu
from jax.sharding import PartitionSpec as P

MESH = pl.DeviceIdType.MESH
LOG2E = 1.4426950408889634
F32, BF16 = jnp.float32, jnp.bfloat16
NZ = 8
UB = 256
US = 512
CH = 128
SLOT = CH + 16
PIECES = ((0, 80), (80, 64))
K = 8
ROWS = 16
BROWS = 32
NT = (((1,), (1,)), ((), ()))


def kernel(
    q_ref, c_ref, gq_ref, gc_ref, slope_ref, t_ref, tgt_ref,
    loss_ref, ug_ref, ig_ref, ugate_ref, igate_ref,
    qall, ugall, call, xstage, gpad_a, gpad_b, git_a, git_b, ctall, qm, gub, tgtb,
    logit_a, logit_b, weight, score, dinv, mx, sm, ps, stat, ltb,
    lg_a, lg_b, igp_a, igp_b, gacc_a, gacc_b, gacc_c, ugv, uacc, ib_a, ib_b, ib_c, qpair, sbuf, rbuf, gsend, grecv,
    urecv, ukeep, usend, uxrecv, isend, irecv, igx, ugsend, ugrecv,
    x_s, x_r, q_s, q_r, u_s, u_r, ag_s, ag_r, st_s, st_r,
    rs_s, rs_r, g_s, g_r, uc_s, uc_r, ux_s, ux_r, fx_s, fx_r, ugs_s, ugs_r,
):
    blk = lax.axis_index("blk")
    x = lax.axis_index("comp")
    z = blk // 2
    c = lax.rem(blk, 2)
    me = 2 * x + c

    def dev(zz, cc, xx):
        return {"blk": lax.rem(zz + NZ, NZ) * 2 + cc, "comp": xx}

    def rc(src, dst, ss, rs, device):
        return pltpu.make_async_remote_copy(
            src_ref=src, dst_ref=dst, send_sem=ss, recv_sem=rs, device_id=device, device_id_type=MESH
        )

    xp, cp, dp = dev(z, c, 1 - x), dev(z, 1 - c, x), dev(z, 1 - c, 1 - x)
    quad = (xp, cp, dp)

    barrier = pltpu.get_barrier_semaphore()
    near = [dev(z + d, c, x) for d in (-2, -1, 1, 2)] + [dev(z + d, c, 1 - x) for d in (-1, 1)]
    for peer in (*quad, *near):
        pl.semaphore_signal(barrier, inc=1, device_id=peer, device_id_type=MESH)

    own_rows = pl.ds(pl.multiple_of(x * CH, CH), CH)
    peer_rows = pl.ds(pl.multiple_of((1 - x) * CH, CH), CH)
    gc = gc_ref[...].astype(F32)
    gc = jnp.concatenate([gc, gc], axis=0)
    gc = jnp.concatenate([gc, gc], axis=0)
    low = jnp.broadcast_to(x, (16, CH)) == 0
    blank = jnp.zeros((16, CH), F32)
    own_gate = jnp.concatenate([jnp.where(low, gc[:, :CH], gc[:, CH:]), blank], axis=1)
    peer_gate = jnp.concatenate([jnp.where(low, gc[:, CH:], gc[:, :CH]), blank], axis=1)
    call[z, x, :CH, :] = c_ref[own_rows, :]
    call[z, x, CH:, :] = own_gate.astype(BF16)
    xstage[:CH, :] = c_ref[peer_rows, :]
    xstage[CH:, :] = peer_gate.astype(BF16)
    qall[c, x] = q_ref[...]
    gq = gq_ref[...].astype(F32)
    ugall[me] = jnp.concatenate([gq, jnp.broadcast_to(tgt_ref[...].astype(F32), (4, UB))], axis=0)

    pl.semaphore_wait(barrier, len(quad) + len(near))

    def hop(dr, s, hh, n):
        step = 1 - 2 * dr
        o = lax.rem(z - step * min(s - 1, 2) + NZ, NZ)
        h = x if hh == 0 else 1 - x
        at = call.at[o, h, pl.ds(*PIECES[n]), :]
        return rc(at, at, ag_s.at[dr, s - 1, hh, n], ag_r.at[dr, s - 1, hh, n],
                  dev(z + (2 * step if s == 4 else step), c, x))

    def arrive(s, halves=(0, 1)):
        for hh in halves:
            for n in range(2):
                for dr in range(2):
                    if s < 4 or hh == dr:
                        hop(dr, s, hh, n).wait_recv()
                    if s == 2 and hh == dr:
                        hop(dr, 4, hh, n).start()
                    if s < 3:
                        hop(dr, s + 1, hh, n).start()

    x_items, q_xs, q_fs = [], [], []
    for n in range(2):
        part = pl.ds(*PIECES[n])
        x_items.append(rc(xstage.at[part, :], call.at[z, x, part, :], x_s.at[n], x_r.at[n], xp))
        part = pl.ds(n * CH, CH)
        q_xs.append(rc(q_ref.at[part, :], qall.at[c, x, part, :], q_s.at[n], q_r.at[n], xp))
        come = qall.at[c, 1 - x, part, :]
        q_fs.append(rc(come, come, q_s.at[3 + n], q_r.at[3 + n], cp))
    q_c = rc(q_ref, qall.at[c, x], q_s.at[2], q_r.at[2], cp)
    u_sends = [rc(ugall.at[me], ugall.at[me], u_s.at[i], u_r.at[i], quad[i]) for i in range(3)]
    for copy in x_items:
        copy.start()
    for n in range(2):
        hop(0, 1, 0, n).start()
        hop(1, 1, 0, n).start()
    for copy in q_xs:
        copy.start()
    for s in u_sends:
        s.start()
    q_c.start()

    gpad_a[...] = jnp.zeros_like(gpad_a)
    gpad_b[...] = jnp.zeros_like(gpad_b)
    mx[...] = jnp.full(mx.shape, -3.0e38, F32)
    sm[...] = jnp.zeros_like(sm)
    ps[...] = jnp.zeros_like(ps)
    uacc[...] = jnp.zeros_like(uacc)
    ugv[...] = jnp.zeros_like(ugv)
    lg_b[...] = jnp.zeros_like(lg_b)
    igp_b[...] = jnp.zeros_like(igp_b)

    for n in range(2):
        x_items[n].wait_recv()
        hop(0, 1, 1, n).start()
        hop(1, 1, 1, n).start()
    for n in range(2):
        q_xs[n].wait_recv()
        q_fs[n].start()
    arrive(1, (0,))

    lane = lax.broadcasted_iota(jnp.int32, (UB, CH), 1)

    def mask_users(cc, h):
        for p in range(2):
            rows = pl.ds(pl.multiple_of(cc * UB, UB), UB)
            k = 4 * h + 2 * p
            qpair[k // 2, rows, :] = qall[cc, h, :, p * CH : (p + 1) * CH]
            pair = qall[cc, h, :, p * CH : (p + 1) * CH].astype(F32)
            qm[k, rows, :] = jnp.where(lane < 64, pair, 0.0).astype(BF16)
            qm[k + 1, rows, :] = jnp.where(lane < 64, 0.0, pair).astype(BF16)

    for h in range(2):
        mask_users(c, h)
    for s in u_sends:
        s.wait_recv()
    for k in range(K):
        h, r = k // 4, k % 4
        row = jnp.concatenate([ugall[2 * h, r : r + 1, :], ugall[2 * h + 1, r : r + 1, :]], axis=1)
        gub[k] = jnp.broadcast_to(row * LOG2E, (8, US))
    tgtb[...] = jnp.broadcast_to(
        jnp.concatenate([ugall[0, 4:5, :], ugall[1, 4:5, :]], axis=1), (8, US)
    )
    q_c.wait_recv()
    for copy in q_fs:
        copy.wait_recv()
    for h in range(2):
        mask_users(1 - c, h)

    inv_t = 1.0 / jnp.full((8, US), t_ref[0], F32)
    scale2 = inv_t * LOG2E

    def twice(v):
        return jnp.concatenate([v, v], axis=0)

    def is_positive(o, r, rows):
        ids = lax.broadcasted_iota(jnp.int32, (rows, US), 0) + (
            (o * 2 + c) * UB + x * CH + r * rows
        )
        return jnp.concatenate([tgtb[...]] * (rows // 8), axis=0) == ids.astype(F32)

    def gates_of(o, gpad, git):
        gpad[0:16, :] = call[o, 0, CH:, :CH].astype(F32)
        gpad[16:32, :] = call[o, 1, CH:, :CH].astype(F32)
        git[...] = gpad[...].T * LOG2E

    def logits_of(o, logit, s, k):
        h, p = k // 4, lax.rem(k, 4) // 2
        at = pl.ds(pl.multiple_of(p * CH, CH), CH)
        logit[s, k] = lax.dot_general(call[o, h, :CH, at], qm[k], NT, preferred_element_type=F32)

    def scores_of(o, logit, s, git, o_next, logit_next, s_next, gpad_next, git_next):
        gates_of(o_next, gpad_next, git_next)
        for h in range(2):
            for p in range(2):
                at = slice((2 * h + p) * CH, (2 * h + p + 1) * CH)
                ctall[o, at, :] = call[o, h, :CH, p * CH : (p + 1) * CH].T

        def rows_of(r, carry):
            top, pos = carry
            logits_of(o_next, logit_next, s_next, r)
            rows = pl.ds(pl.multiple_of(r * ROWS, ROWS), ROWS)
            den = num = None
            gcols = git[rows, :]
            for k in range(K):
                col = (k // 4) * 16 + k % 4
                l = logit[s, k, rows, :]
                e = jnp.tanh(l) * (slope_ref[k] * LOG2E) + gcols[:, col : col + 1] + twice(gub[k])
                w = jnp.exp2(e)
                weight[o, k, rows, :] = w
                wl = w * l
                den = w if den is None else den + w
                num = wl if num is None else num + wl
            di = 1.0 / den
            sc = num * di
            dinv[o, rows, :] = di
            score[o, rows, :] = sc
            hit = jnp.where(is_positive(o, r, ROWS), sc, 0.0)
            return (
                jnp.maximum(top, jnp.maximum(sc[:8], sc[8:])),
                pos + hit[:8] + hit[8:],
            )

        before = mx[...]
        top, pos = lax.fori_loop(0, CH // ROWS, rows_of, (before, ps[...]), unroll=True)
        mx[...] = top
        ps[...] = pos
        shift = top * scale2
        total = sm[...] * jnp.exp2((before - top) * scale2)
        for m in range(CH // 8):
            total = total + jnp.exp2(score[o, m * 8 : (m + 1) * 8, :] * scale2 - shift)
        sm[...] = total

    arrive(1, (1,))
    gates_of(z, gpad_a, git_a)

    def own_logits(k, carry):
        logits_of(z, logit_a, 0, k)
        return carry

    lax.fori_loop(0, K, own_logits, 0, unroll=True)

    def forward(i, carry):
        for s in (2, 3, 4):

            @pl.when(i == s - 1)
            def _():
                arrive(s)

        left = lax.rem(z + NZ - i, NZ)
        right = lax.rem(z + i + 1, NZ)
        after = jnp.minimum(i + 1, 3)
        scores_of(left, logit_a, i, git_a, right, logit_b, i, gpad_b, git_b)
        scores_of(
            right, logit_b, i, git_b, lax.rem(z + NZ - after, NZ), logit_a, after, gpad_a, git_a
        )
        return carry

    lax.fori_loop(0, NZ // 2, forward, 0)

    top = jnp.max(mx[...], axis=0, keepdims=True)
    total = sm[...] * jnp.exp2((mx[...] - top) * scale2)
    stat[me] = jnp.concatenate(
        [
            top,
            jnp.sum(total, axis=0, keepdims=True),
            jnp.sum(ps[...], axis=0, keepdims=True),
            jnp.zeros((5, US), F32),
        ],
        axis=0,
    )
    st_sends = [rc(stat.at[me], stat.at[me], st_s.at[i], st_r.at[i], quad[i]) for i in range(3)]
    for s in st_sends:
        s.start()
    for s in st_sends:
        s.wait_recv()
    st = [stat[i] for i in range(4)]
    all_top = jnp.maximum(jnp.maximum(st[0][0:1], st[1][0:1]), jnp.maximum(st[2][0:1], st[3][0:1]))
    inv_row = inv_t[0:1]
    all_sum = all_pos = None
    for i in range(4):
        part = st[i][1:2] * jnp.exp((st[i][0:1] - all_top) * inv_row)
        all_sum = part if all_sum is None else all_sum + part
        all_pos = st[i][2:3] if all_pos is None else all_pos + st[i][2:3]
    log_total = all_top * inv_row + jnp.log(all_sum)
    loss = log_total - all_pos * inv_row
    loss_ref[...] = jnp.where(jnp.broadcast_to(c, (1, UB)) == 0, loss[:, :UB], loss[:, UB:])
    ltb[...] = jnp.broadcast_to(log_total * LOG2E, (8, US))

    ones_row = lax.broadcasted_iota(jnp.int32, (8, 2 * CH), 0)
    ones_col = lax.broadcasted_iota(jnp.int32, (8, 2 * CH), 1) // CH
    ones = jnp.where(ones_row == ones_col, 1.0, 0.0).astype(BF16)

    def gate_copy(dr, d):
        far = 2 if d == 4 else 1
        return rc(
            gsend.at[dr, d - 1], grecv.at[dr, d - 1], g_s.at[dr, d - 1], g_r.at[dr, d - 1],
            dev(z + far * (2 * dr - 1), c, x),
        )

    def rs_copy(dr, d, h):
        far = 2 if d == 4 else 1
        return rc(
            sbuf.at[dr, d - 1, h], rbuf.at[dr, d - 1, h], rs_s.at[dr, d - 1, h], rs_r.at[dr, d - 1, h],
            dev(z + far * (2 * dr - 1), c, x),
        )

    def last_copy(dr, w):
        h = x if w == 0 else 1 - x
        return rc(
            sbuf.at[dr, 0, h], rbuf.at[dr, 0, w], rs_s.at[dr, 0, w], rs_r.at[dr, 0, w],
            dev(z + 2 * dr - 1, c, h),
        )

    def matmuls(o, lg, igp, ib, gacc, r):
        both = jnp.dot(
            lg[pl.ds(pl.multiple_of(r * 2 * CH, 2 * CH), 2 * CH), :], qpair[r], preferred_element_type=F32
        )
        ib[r] = jnp.where(lane[:CH] < 64, both[:CH], both[CH:])
        for kk in range(2):
            at = pl.ds(pl.multiple_of(r * CH + kk * 64, 64), 64)
            part = jnp.dot(
                ctall[o, at, :],
                lg[pl.ds(pl.multiple_of((2 * r + kk) * CH, CH), CH), :],
                preferred_element_type=F32,
            )
            uacc[0, at, :] += part[:, :UB]
            uacc[1, at, :] += part[:, UB:]
        gates = igp[r]
        hi = gates.astype(BF16)
        lo = (gates - hi.astype(F32)).astype(BF16)
        gacc[r] = lax.dot_general(ones, hi, NT, preferred_element_type=F32) + lax.dot_general(
            ones, lo, NT, preferred_element_type=F32
        )

    def item_sum(ib, h):
        return jnp.concatenate([ib[2 * h], ib[2 * h + 1]], axis=1)

    def gate_sum(gacc):
        return jnp.concatenate([gacc[i, 0:2, :] for i in range(4)], axis=0)

    def four(v):
        return jnp.concatenate([v] * (BROWS // 8), axis=0)

    def chunk(o, logit, s, lg, igp, o_before, lg_before, igp_before, ib, gacc):
        def rows_of(r, carry):
            rows = pl.ds(pl.multiple_of(r * BROWS, BROWS), BROWS)
            matmuls(o_before, lg_before, igp_before, ib, gacc, r)
            sc = score[o, rows, :]
            soft = jnp.exp2(sc * four(scale2) - four(ltb[...]))
            soft = jnp.where(is_positive(o, r, BROWS), soft - 1.0, soft) * four(inv_t)
            share = soft * dinv[o, rows, :]
            for k in range(K):
                l = logit[s, k, rows, :]
                t = jnp.tanh(l)
                g = weight[o, k, rows, :] * share
                gg = g * (l - sc)
                sk = slope_ref[k]
                out = g + gg * (sk - (t * t) * sk)
                lg[pl.ds(pl.multiple_of(k * CH + r * BROWS, BROWS), BROWS), :] = out.astype(BF16)
                ugv[k] = ugv[k] + ((gg[:8] + gg[8:16]) + (gg[16:24] + gg[24:]))
                igp[k // 2, rows, (k % 2) * CH : (k % 2 + 1) * CH] = (
                    gg[:, 0:128] + gg[:, 128:256]
                ) + (gg[:, 256:384] + gg[:, 384:512])
            return carry

        lax.fori_loop(0, CH // BROWS, rows_of, 0, unroll=True)

    def send(dr, d, ib, gacc):
        if d == 3:
            for h in range(2):
                sbuf[dr, 2, h] = item_sum(ib, h).astype(BF16)
                rs_copy(dr, 3, h).start()
            gsend[dr, 2] = gate_sum(gacc)
            gate_copy(dr, 3).start()
        elif d == 2:
            for h in range(2):
                rs_copy(dr, 3, h).wait_recv()
                value = item_sum(ib, h) + rbuf[dr, 2, h].astype(F32)
                if h == dr:
                    rs_copy(dr, 4, h).wait_recv()
                    value = value + rbuf[dr, 3, h].astype(F32)
                sbuf[dr, 1, h] = value.astype(BF16)
                rs_copy(dr, 2, h).start()
            gate_copy(dr, 3).wait_recv()
            value = gate_sum(gacc) + grecv[dr, 2]
            if dr == 0:
                gate_copy(0, 4).wait_recv()
                value = value + grecv[0, 3]
            gsend[dr, 1] = value
            gate_copy(dr, 2).start()
        else:
            for h in range(2):
                rs_copy(dr, 2, h).wait_recv()
                sbuf[dr, 0, h] = (item_sum(ib, h) + rbuf[dr, 1, h].astype(F32)).astype(BF16)
            for w in (1, 0):
                last_copy(dr, w).start()
            gate_copy(dr, 2).wait_recv()
            gsend[dr, 0] = gate_sum(gacc) + grecv[dr, 1]
            gate_copy(dr, 1).start()

    def backward(jj, carry):
        d = 4 - jj
        right = lax.rem(z + d, NZ)
        chunk(
            right, logit_b, d - 1, lg_a, igp_a, lax.rem(z + NZ - d, NZ), lg_b, igp_b, ib_a, gacc_a
        )
        for dd in (3, 2):

            @pl.when(d == dd)
            def _():
                send(0, dd, ib_a, gacc_a)

        left = lax.rem(z + NZ - (d - 1), NZ)
        chunk(left, logit_a, d - 1, lg_b, igp_b, right, lg_a, igp_a, ib_b, gacc_b)

        @pl.when(d == 4)
        def _():
            for h in range(2):
                sbuf[h, 3, h] = item_sum(ib_b, h).astype(BF16)
                rs_copy(h, 4, h).start()
            gsend[0, 3] = gate_sum(gacc_b)
            gate_copy(0, 4).start()

        for dd in (3, 2):

            @pl.when(d == dd)
            def _():
                send(1, dd, ib_b, gacc_b)

        return carry

    lax.fori_loop(0, NZ // 2, backward, 0)
    send(0, 1, ib_a, gacc_a)

    def u_core(hh, p):
        h = 1 - x if hh == 0 else x
        at = pl.ds(pl.multiple_of(h * UB + p * CH, CH), CH)
        return rc(uacc.at[1 - c, at, :], urecv.at[hh, p], uc_s.at[hh, p], uc_r.at[hh, p], cp)

    def u_x(p):
        return rc(usend.at[p], uxrecv.at[p], ux_s.at[p], ux_r.at[p], xp)

    def core_sum(hh, p):
        h = 1 - x if hh == 0 else x
        at = pl.ds(pl.multiple_of(h * UB + p * CH, CH), CH)
        u_core(hh, p).wait_recv()
        return uacc[c, at, :] + urecv[hh, p]

    for hh in range(2):
        for p in range(2):
            h = 1 - x if hh == 0 else x
            matmuls(z, lg_b, igp_b, ib_c, gacc_c, 2 * h + p)
            u_core(hh, p).start()
    send(1, 1, ib_b, gacc_b)
    for p in range(2):
        usend[p] = core_sum(0, p).astype(BF16)
        u_x(p).start()

    sums = [item_sum(ib_c, h) for h in range(2)]
    first = jnp.broadcast_to(x, (CH, UB)) == 0
    isend[...] = jnp.where(first, sums[1], sums[0]).astype(BF16)
    keep = jnp.where(first, sums[0], sums[1])
    i_x = rc(isend, irecv, fx_s.at[0], fx_r.at[0], xp)
    i_x.start()
    for k in range(K):
        ugsend[k : k + 1, :] = jnp.sum(ugv[k], axis=0, keepdims=True)
    ug_sends = [rc(ugsend, ugrecv.at[i], ugs_s.at[i], ugs_r.at[i], quad[i]) for i in range(3)]
    for s in ug_sends:
        s.start()
    gate = gate_sum(gacc_c)
    for dr in range(2):
        gate_copy(dr, 1).wait_recv()
        gate = gate + grecv[dr, 0]
    igx[0] = gate
    ig_x = rc(igx.at[0], igx.at[1], fx_s.at[1], fx_r.at[1], xp)
    ig_x.start()

    for p in range(2):
        ukeep[p * CH : (p + 1) * CH, :] = core_sum(1, p)
    for s in ug_sends:
        s.wait_recv()
    ugate = (ugsend[...] + ugrecv[0]) + (ugrecv[1] + ugrecv[2])
    ugate = jnp.where(jnp.broadcast_to(c, (K, UB)) == 0, ugate[:, :UB], ugate[:, UB:])
    ugate_ref[...] = jnp.where(jnp.broadcast_to(x, (4, UB)) == 0, ugate[:4], ugate[4:])

    for dr in range(2):
        last_copy(dr, 0).wait_recv()
    ig_ref[own_rows, :] = keep + (rbuf[0, 0, 0].astype(F32) + rbuf[1, 0, 0].astype(F32))
    for dr in range(2):
        last_copy(dr, 1).wait_recv()
    i_x.wait_recv()
    ig_ref[peer_rows, :] = irecv[...].astype(F32) + (
        rbuf[0, 0, 1].astype(F32) + rbuf[1, 0, 1].astype(F32)
    )
    ig_x.wait_recv()
    mine, theirs = igx[0], igx[1]
    upper = jnp.concatenate([mine, theirs], axis=1)[:4]
    lower = jnp.concatenate([theirs, mine], axis=1)[4:]
    igate_ref[...] = jnp.where(jnp.broadcast_to(x, (4, UB)) == 0, upper, lower)
    for p in range(2):
        u_x(p).wait_recv()
        at = slice(p * CH, (p + 1) * CH)
        ug_ref[:, at] = (ukeep[at, :] + uxrecv[p].astype(F32)).T

    for s in (*x_items, *q_xs, q_c, *q_fs, *u_sends, *st_sends, i_x, ig_x, *ug_sends):
        s.wait_send()
    for p in range(2):
        u_x(p).wait_send()
        for hh in range(2):
            u_core(hh, p).wait_send()
    gate_copy(0, 4).wait_send()
    for dr in range(2):
        rs_copy(dr, 4, dr).wait_send()
        for d in (1, 2, 3):
            gate_copy(dr, d).wait_send()
        for w in range(2):
            last_copy(dr, w).wait_send()
            for d in (2, 3):
                rs_copy(dr, d, w).wait_send()
        for hh in range(2):
            for s in range(1, 5 if hh == dr else 4):
                for n in range(2):
                    hop(dr, s, hh, n).wait_send()


def write_out(*refs):
    ins, outs, held, in_sem, out_sem = refs[:5], refs[5:10], refs[10:15], refs[15], refs[16]
    come = [pltpu.make_async_copy(ins[i], held[i], in_sem.at[i]) for i in range(5)]
    leave = [pltpu.make_async_copy(held[i], outs[i], out_sem.at[i]) for i in range(5)]
    for i in (1, 2, 0, 3, 4):
        come[i].start()
    for i in (1, 2, 0, 3, 4):
        come[i].wait()
        leave[i].start()
    for copy in leave:
        copy.wait()


def body(query, candidate, query_gate, candidate_gate, slope, scale, target):
    vmem = pl.BlockSpec(memory_space=pltpu.VMEM)
    smem = pl.BlockSpec(memory_space=pltpu.SMEM)
    hbm = pl.BlockSpec(memory_space=pl.ANY)
    dma = pltpu.SemaphoreType.DMA
    scratch = [
        pltpu.VMEM((2, 2, UB, UB), BF16),
        pltpu.VMEM((4, 8, UB), F32),
        pltpu.VMEM((NZ, 2, SLOT, UB), BF16),
        pltpu.VMEM((SLOT, UB), BF16),
        pltpu.VMEM((CH, CH), F32),
        pltpu.VMEM((CH, CH), F32),
        pltpu.VMEM((CH, CH), F32),
        pltpu.VMEM((CH, CH), F32),
        pltpu.VMEM((NZ, K * 64, CH), BF16),
        pltpu.VMEM((K, US, CH), BF16),
        pltpu.VMEM((K, 8, US), F32),
        pltpu.VMEM((8, US), F32),
        pltpu.VMEM((NZ // 2, K, CH, US), F32),
        pltpu.VMEM((NZ // 2, K, CH, US), F32),
        pltpu.VMEM((NZ, K, CH, US), F32),
        pltpu.VMEM((NZ, CH, US), F32),
        pltpu.VMEM((NZ, CH, US), F32),
        pltpu.VMEM((8, US), F32),
        pltpu.VMEM((8, US), F32),
        pltpu.VMEM((8, US), F32),
        pltpu.VMEM((4, 8, US), F32),
        pltpu.VMEM((8, US), F32),
        pltpu.VMEM((K * CH, US), BF16),
        pltpu.VMEM((K * CH, US), BF16),
        pltpu.VMEM((4, CH, 2 * CH), F32),
        pltpu.VMEM((4, CH, 2 * CH), F32),
        pltpu.VMEM((4, 8, CH), F32),
        pltpu.VMEM((4, 8, CH), F32),
        pltpu.VMEM((4, 8, CH), F32),
        pltpu.VMEM((K, 8, US), F32),
        pltpu.VMEM((2, US, UB), F32),
        pltpu.VMEM((4, CH, CH), F32),
        pltpu.VMEM((4, CH, CH), F32),
        pltpu.VMEM((4, CH, CH), F32),
        pltpu.VMEM((4, US, CH), BF16),
        pltpu.VMEM((2, 4, 2, CH, UB), BF16),
        pltpu.VMEM((2, 4, 2, CH, UB), BF16),
        pltpu.VMEM((2, 4, K, CH), F32),
        pltpu.VMEM((2, 4, K, CH), F32),
        pltpu.VMEM((2, 2, CH, UB), F32),
        pltpu.VMEM((UB, UB), F32),
        pltpu.VMEM((2, CH, UB), BF16),
        pltpu.VMEM((2, CH, UB), BF16),
        pltpu.VMEM((CH, UB), BF16),
        pltpu.VMEM((CH, UB), BF16),
        pltpu.VMEM((2, K, CH), F32),
        pltpu.VMEM((K, US), F32),
        pltpu.VMEM((3, K, US), F32),
        dma((2,)), dma((2,)),
        dma((5,)), dma((5,)),
        dma((3,)), dma((3,)),
        dma((2, 4, 2, 2)), dma((2, 4, 2, 2)),
        dma((3,)), dma((3,)),
        dma((2, 4, 2)), dma((2, 4, 2)),
        dma((2, 4)), dma((2, 4)),
        dma((2, 2)), dma((2, 2)),
        dma((2,)), dma((2,)),
        dma((2,)), dma((2,)),
        dma((3,)), dma((3,)),
    ]
    outs = (
        jax.ShapeDtypeStruct((1, UB), F32),
        jax.ShapeDtypeStruct((UB, UB), F32),
        jax.ShapeDtypeStruct((UB, UB), F32),
        jax.ShapeDtypeStruct((4, UB), F32),
        jax.ShapeDtypeStruct((4, UB), F32),
    )
    results = pl.pallas_call(
        kernel,
        out_shape=outs,
        in_specs=[vmem, vmem, vmem, vmem, smem, smem, vmem],
        out_specs=(vmem,) * 5,
        scratch_shapes=scratch,
        compiler_params=pltpu.CompilerParams(
            collective_id=0, has_side_effects=True, vmem_limit_bytes=60 * 1024 * 1024
        ),
    )(query, candidate, query_gate, candidate_gate, slope, scale, target.reshape(1, UB))
    loss, ug, ig, ugate, igate = pl.pallas_call(
        write_out,
        out_shape=outs,
        in_specs=[hbm] * 5,
        out_specs=(hbm,) * 5,
        scratch_shapes=[*(pltpu.VMEM(out.shape, F32) for out in outs), dma((5,)), dma((5,))],
    )(*results)
    return loss.reshape(UB), ug, ig, ugate, igate


def solution(mesh):
    in_specs = (
        P(("task", "blk"), "comp"),
        P(("task", "blk"), "comp"),
        P("comp", ("task", "blk")),
        P("comp", ("task", "blk")),
        P(),
        P("task"),
        P(("task", "blk")),
    )
    out_specs = (
        P(("task", "blk")),
        P(("task", "blk"), "comp"),
        P(("task", "blk"), "comp"),
        P("comp", ("task", "blk")),
        P("comp", ("task", "blk")),
    )
    return jax.shard_map(body, mesh=mesh, in_specs=in_specs, out_specs=out_specs, check_vma=False)
```

```python
import jax
import jax.numpy as jnp
from jax import lax
from jax.experimental import pallas as pl
from jax.experimental.pallas import tpu as pltpu
from jax.sharding import PartitionSpec as P

MESH = pl.DeviceIdType.MESH
LOG2E = 1.4426950408889634
F32, BF16 = jnp.float32, jnp.bfloat16
NZ = 8
UB = 256
US = 512
CH = 128
SLOT = CH + 16
PIECES = (((0, 64), (64, 64)), ((0, 80), (80, 64)))
K = 8
ROWS = 16
BROWS = 32
NT = (((1,), (1,)), ((), ()))


def kernel(
    q_ref, c_ref, gq_ref, gc_ref, slope_ref, t_ref, tgt_ref,
    loss_ref, ug_ref, ig_ref, ugate_ref, igate_ref,
    qall, ugall, call, xstage, gpad_a, gpad_b, git_a, git_b, ctall, qm, gub, tgtb,
    logit_a, logit_b, weight, score, dinv, mx, sm, ps, stat, ltb,
    lg_a, lg_b, igp_a, igp_b, gacc, ugv, uacc, ib, qpair, sbuf, rbuf, gsend, grecv,
    urecv, ukeep, usend, uxrecv, isend, irecv, igx, ugsend, ugrecv,
    x_s, x_r, q_s, q_r, u_s, u_r, ag_s, ag_r, st_s, st_r,
    rs_s, rs_r, g_s, g_r, uc_s, uc_r, ux_s, ux_r, fx_s, fx_r, ugs_s, ugs_r,
):
    blk = lax.axis_index("blk")
    x = lax.axis_index("comp")
    z = blk // 2
    c = lax.rem(blk, 2)
    me = 2 * x + c

    def dev(zz, cc, xx):
        return {"blk": lax.rem(zz + NZ, NZ) * 2 + cc, "comp": xx}

    def rc(src, dst, ss, rs, device):
        return pltpu.make_async_remote_copy(
            src_ref=src, dst_ref=dst, send_sem=ss, recv_sem=rs, device_id=device, device_id_type=MESH
        )

    xp, cp, dp = dev(z, c, 1 - x), dev(z, 1 - c, x), dev(z, 1 - c, 1 - x)
    quad = (xp, cp, dp)

    barrier = pltpu.get_barrier_semaphore()
    near = [dev(z + d, c, x) for d in (-2, -1, 1, 2)] + [dev(z + d, c, 1 - x) for d in (-1, 1)]
    for peer in (*quad, *near):
        pl.semaphore_signal(barrier, inc=1, device_id=peer, device_id_type=MESH)

    own_rows = pl.ds(pl.multiple_of(x * CH, CH), CH)
    peer_rows = pl.ds(pl.multiple_of((1 - x) * CH, CH), CH)
    gc = gc_ref[...].astype(F32)
    gc = jnp.concatenate([gc, gc], axis=0)
    gc = jnp.concatenate([gc, gc], axis=0)
    low = jnp.broadcast_to(x, (16, CH)) == 0
    blank = jnp.zeros((16, CH), F32)
    own_gate = jnp.where(low, gc[:, :CH], gc[:, CH:]).astype(BF16)
    peer_gate = jnp.concatenate([jnp.where(low, gc[:, CH:], gc[:, :CH]), blank], axis=1)
    call[z, x, :CH, :] = c_ref[own_rows, :]
    xstage[:CH, :] = c_ref[peer_rows, :]
    xstage[CH:, :] = peer_gate.astype(BF16)
    qall[c, x] = q_ref[...]
    gq = gq_ref[...].astype(F32)
    ugall[me] = jnp.concatenate([gq, jnp.broadcast_to(tgt_ref[...].astype(F32), (4, UB))], axis=0)

    pl.semaphore_wait(barrier, len(quad) + len(near))

    def hop(dr, s, hh, n):
        step = 1 - 2 * dr
        o = lax.rem(z - step * min(s - 1, 2) + NZ, NZ)
        h = x if hh == 0 else 1 - x
        at = call.at[o, h, pl.ds(*PIECES[hh][n]), :]
        return rc(at, at, ag_s.at[dr, s - 1, hh, n], ag_r.at[dr, s - 1, hh, n],
                  dev(z + (2 * step if s == 4 else step), c, x))

    def arrive(s, halves=(0, 1)):
        for hh in halves:
            for n in range(2):
                for dr in range(2):
                    if s < 4 or hh == dr:
                        hop(dr, s, hh, n).wait_recv()
                    if s == 2 and hh == dr:
                        hop(dr, 4, hh, n).start()
                    if s < 3:
                        hop(dr, s + 1, hh, n).start()

    x_item = rc(xstage, call.at[z, x], x_s.at[0], x_r.at[0], xp)
    q_x = rc(q_ref, qall.at[c, x], q_s.at[0], q_r.at[0], xp)
    q_c = rc(q_ref, qall.at[c, x], q_s.at[1], q_r.at[1], cp)
    q_f = rc(qall.at[c, 1 - x], qall.at[c, 1 - x], q_s.at[2], q_r.at[2], cp)
    u_sends = [rc(ugall.at[me], ugall.at[me], u_s.at[i], u_r.at[i], quad[i]) for i in range(3)]
    x_item.start()
    for n in range(2):
        hop(0, 1, 0, n).start()
        hop(1, 1, 0, n).start()
    q_x.start()
    for s in u_sends:
        s.start()
    q_c.start()

    gpad_a[...] = jnp.zeros_like(gpad_a)
    gpad_b[...] = jnp.zeros_like(gpad_b)
    mx[...] = jnp.full(mx.shape, -3.0e38, F32)
    sm[...] = jnp.zeros_like(sm)
    ps[...] = jnp.zeros_like(ps)
    uacc[...] = jnp.zeros_like(uacc)
    ugv[...] = jnp.zeros_like(ugv)
    lg_b[...] = jnp.zeros_like(lg_b)
    igp_b[...] = jnp.zeros_like(igp_b)

    x_item.wait_recv()
    call[z, 1 - x, CH:, CH:] = own_gate
    for n in range(2):
        hop(0, 1, 1, n).start()
        hop(1, 1, 1, n).start()
    q_x.wait_recv()
    q_f.start()
    arrive(1, (0,))

    lane = lax.broadcasted_iota(jnp.int32, (UB, CH), 1)

    def mask_users(cc, h):
        for p in range(2):
            rows = pl.ds(pl.multiple_of(cc * UB, UB), UB)
            k = 4 * h + 2 * p
            qpair[k // 2, rows, :] = qall[cc, h, :, p * CH : (p + 1) * CH]
            pair = qall[cc, h, :, p * CH : (p + 1) * CH].astype(F32)
            qm[k, rows, :] = jnp.where(lane < 64, pair, 0.0).astype(BF16)
            qm[k + 1, rows, :] = jnp.where(lane < 64, 0.0, pair).astype(BF16)

    for h in range(2):
        mask_users(c, h)
    for s in u_sends:
        s.wait_recv()
    for k in range(K):
        h, r = k // 4, k % 4
        row = jnp.concatenate([ugall[2 * h, r : r + 1, :], ugall[2 * h + 1, r : r + 1, :]], axis=1)
        gub[k] = jnp.broadcast_to(row * LOG2E, (8, US))
    tgtb[...] = jnp.broadcast_to(
        jnp.concatenate([ugall[0, 4:5, :], ugall[1, 4:5, :]], axis=1), (8, US)
    )
    q_c.wait_recv()
    q_f.wait_recv()
    for h in range(2):
        mask_users(1 - c, h)

    inv_t = 1.0 / jnp.full((8, US), t_ref[0], F32)
    scale2 = inv_t * LOG2E

    def twice(v):
        return jnp.concatenate([v, v], axis=0)

    def is_positive(o, r, rows):
        ids = lax.broadcasted_iota(jnp.int32, (rows, US), 0) + (
            (o * 2 + c) * UB + x * CH + r * rows
        )
        return jnp.concatenate([tgtb[...]] * (rows // 8), axis=0) == ids.astype(F32)

    def gates_of(o, gpad, git):
        gates = call[o, 1 - x, CH:, :].astype(F32)
        gpad[pl.ds(pl.multiple_of((1 - x) * 16, 16), 16), :] = gates[:, :CH]
        gpad[pl.ds(pl.multiple_of(x * 16, 16), 16), :] = gates[:, CH:]
        git[...] = gpad[...].T * LOG2E

    def logits_of(o, logit, s, k):
        h, p = k // 4, lax.rem(k, 4) // 2
        at = pl.ds(pl.multiple_of(p * CH, CH), CH)
        logit[s, k] = lax.dot_general(call[o, h, :CH, at], qm[k], NT, preferred_element_type=F32)

    def scores_of(o, logit, s, git, o_next, logit_next, s_next, gpad_next, git_next):
        gates_of(o_next, gpad_next, git_next)
        for h in range(2):
            for p in range(2):
                at = slice((2 * h + p) * CH, (2 * h + p + 1) * CH)
                ctall[o, at, :] = call[o, h, :CH, p * CH : (p + 1) * CH].T

        def rows_of(r, carry):
            top, pos = carry
            logits_of(o_next, logit_next, s_next, r)
            rows = pl.ds(pl.multiple_of(r * ROWS, ROWS), ROWS)
            den = num = None
            gcols = git[rows, :]
            for k in range(K):
                col = (k // 4) * 16 + k % 4
                l = logit[s, k, rows, :]
                e = jnp.tanh(l) * (slope_ref[k] * LOG2E) + gcols[:, col : col + 1] + twice(gub[k])
                w = jnp.exp2(e)
                weight[o, k, rows, :] = w
                wl = w * l
                den = w if den is None else den + w
                num = wl if num is None else num + wl
            di = 1.0 / den
            sc = num * di
            dinv[o, rows, :] = di
            score[o, rows, :] = sc
            hit = jnp.where(is_positive(o, r, ROWS), sc, 0.0)
            return (
                jnp.maximum(top, jnp.maximum(sc[:8], sc[8:])),
                pos + hit[:8] + hit[8:],
            )

        before = mx[...]
        top, pos = lax.fori_loop(0, CH // ROWS, rows_of, (before, ps[...]), unroll=True)
        mx[...] = top
        ps[...] = pos
        shift = top * scale2
        total = sm[...] * jnp.exp2((before - top) * scale2)
        for m in range(CH // 8):
            total = total + jnp.exp2(score[o, m * 8 : (m + 1) * 8, :] * scale2 - shift)
        sm[...] = total

    arrive(1, (1,))
    gates_of(z, gpad_a, git_a)

    def own_logits(k, carry):
        logits_of(z, logit_a, 0, k)
        return carry

    lax.fori_loop(0, K, own_logits, 0, unroll=True)

    def forward(i, carry):
        for s in (2, 3, 4):

            @pl.when(i == s - 1)
            def _():
                arrive(s)

        left = lax.rem(z + NZ - i, NZ)
        right = lax.rem(z + i + 1, NZ)
        after = jnp.minimum(i + 1, 3)
        scores_of(left, logit_a, i, git_a, right, logit_b, i, gpad_b, git_b)
        scores_of(
            right, logit_b, i, git_b, lax.rem(z + NZ - after, NZ), logit_a, after, gpad_a, git_a
        )
        return carry

    lax.fori_loop(0, NZ // 2, forward, 0)

    top = jnp.max(mx[...], axis=0, keepdims=True)
    total = sm[...] * jnp.exp2((mx[...] - top) * scale2)
    stat[me] = jnp.concatenate(
        [
            top,
            jnp.sum(total, axis=0, keepdims=True),
            jnp.sum(ps[...], axis=0, keepdims=True),
            jnp.zeros((5, US), F32),
        ],
        axis=0,
    )
    st_sends = [rc(stat.at[me], stat.at[me], st_s.at[i], st_r.at[i], quad[i]) for i in range(3)]
    for s in st_sends:
        s.start()
    for s in st_sends:
        s.wait_recv()
    st = [stat[i] for i in range(4)]
    all_top = jnp.maximum(jnp.maximum(st[0][0:1], st[1][0:1]), jnp.maximum(st[2][0:1], st[3][0:1]))
    inv_row = inv_t[0:1]
    all_sum = all_pos = None
    for i in range(4):
        part = st[i][1:2] * jnp.exp((st[i][0:1] - all_top) * inv_row)
        all_sum = part if all_sum is None else all_sum + part
        all_pos = st[i][2:3] if all_pos is None else all_pos + st[i][2:3]
    log_total = all_top * inv_row + jnp.log(all_sum)
    loss = log_total - all_pos * inv_row
    loss_ref[...] = jnp.where(jnp.broadcast_to(c, (1, UB)) == 0, loss[:, :UB], loss[:, UB:])
    ltb[...] = jnp.broadcast_to(log_total * LOG2E, (8, US))

    ones_row = lax.broadcasted_iota(jnp.int32, (8, 2 * CH), 0)
    ones_col = lax.broadcasted_iota(jnp.int32, (8, 2 * CH), 1) // CH
    ones = jnp.where(ones_row == ones_col, 1.0, 0.0).astype(BF16)

    def gate_copy(dr, d):
        far = 2 if d == 4 else 1
        return rc(
            gsend.at[dr, d - 1], grecv.at[dr, d - 1], g_s.at[dr, d - 1], g_r.at[dr, d - 1],
            dev(z + far * (2 * dr - 1), c, x),
        )

    def rs_copy(dr, d, h):
        far = 2 if d == 4 else 1
        return rc(
            sbuf.at[dr, d - 1, h], rbuf.at[dr, d - 1, h], rs_s.at[dr, d - 1, h], rs_r.at[dr, d - 1, h],
            dev(z + far * (2 * dr - 1), c, x),
        )

    def last_copy(dr, w):
        h = x if w == 0 else 1 - x
        return rc(
            sbuf.at[dr, 0, h], rbuf.at[dr, 0, w], rs_s.at[dr, 0, w], rs_r.at[dr, 0, w],
            dev(z + 2 * dr - 1, c, h),
        )

    def matmuls(o, lg, igp, r):
        both = jnp.dot(
            lg[pl.ds(pl.multiple_of(r * 2 * CH, 2 * CH), 2 * CH), :], qpair[r], preferred_element_type=F32
        )
        ib[r] = jnp.where(lane[:CH] < 64, both[:CH], both[CH:])
        for kk in range(2):
            at = pl.ds(pl.multiple_of(r * CH + kk * 64, 64), 64)
            part = jnp.dot(
                ctall[o, at, :],
                lg[pl.ds(pl.multiple_of((2 * r + kk) * CH, CH), CH), :],
                preferred_element_type=F32,
            )
            uacc[0, at, :] += part[:, :UB]
            uacc[1, at, :] += part[:, UB:]
        gates = igp[r]
        hi = gates.astype(BF16)
        lo = (gates - hi.astype(F32)).astype(BF16)
        gacc[r] = lax.dot_general(ones, hi, NT, preferred_element_type=F32) + lax.dot_general(
            ones, lo, NT, preferred_element_type=F32
        )

    def item_sum(h):
        return jnp.concatenate([ib[2 * h], ib[2 * h + 1]], axis=1)

    def gate_sum():
        return jnp.concatenate([gacc[i, 0:2, :] for i in range(4)], axis=0)

    def four(v):
        return jnp.concatenate([v] * (BROWS // 8), axis=0)

    def chunk(o, logit, s, lg, igp, o_before, lg_before, igp_before):
        def rows_of(r, carry):
            rows = pl.ds(pl.multiple_of(r * BROWS, BROWS), BROWS)
            matmuls(o_before, lg_before, igp_before, r)
            sc = score[o, rows, :]
            soft = jnp.exp2(sc * four(scale2) - four(ltb[...]))
            soft = jnp.where(is_positive(o, r, BROWS), soft - 1.0, soft) * four(inv_t)
            share = soft * dinv[o, rows, :]
            for k in range(K):
                l = logit[s, k, rows, :]
                t = jnp.tanh(l)
                g = weight[o, k, rows, :] * share
                gg = g * (l - sc)
                sk = slope_ref[k]
                out = g + gg * (sk - (t * t) * sk)
                lg[pl.ds(pl.multiple_of(k * CH + r * BROWS, BROWS), BROWS), :] = out.astype(BF16)
                ugv[k] = ugv[k] + ((gg[:8] + gg[8:16]) + (gg[16:24] + gg[24:]))
                igp[k // 2, rows, (k % 2) * CH : (k % 2 + 1) * CH] = (
                    gg[:, 0:128] + gg[:, 128:256]
                ) + (gg[:, 256:384] + gg[:, 384:512])
            return carry

        lax.fori_loop(0, CH // BROWS, rows_of, 0, unroll=True)

    def send(dr, jj):
        @pl.when(jj == 1)
        def _():
            for h in range(2):
                sbuf[dr, 2, h] = item_sum(h).astype(BF16)
                rs_copy(dr, 3, h).start()
            gsend[dr, 2] = gate_sum()
            gate_copy(dr, 3).start()

        @pl.when(jj == 2)
        def _():
            for h in range(2):
                rs_copy(dr, 3, h).wait_recv()
                value = item_sum(h) + rbuf[dr, 2, h].astype(F32)
                if h == dr:
                    rs_copy(dr, 4, h).wait_recv()
                    value = value + rbuf[dr, 3, h].astype(F32)
                sbuf[dr, 1, h] = value.astype(BF16)
                rs_copy(dr, 2, h).start()
            gate_copy(dr, 3).wait_recv()
            value = gate_sum() + grecv[dr, 2]
            if dr == 0:
                gate_copy(0, 4).wait_recv()
                value = value + grecv[0, 3]
            gsend[dr, 1] = value
            gate_copy(dr, 2).start()

        @pl.when(jj == 3)
        def _():
            for h in range(2):
                rs_copy(dr, 2, h).wait_recv()
                sbuf[dr, 0, h] = (item_sum(h) + rbuf[dr, 1, h].astype(F32)).astype(BF16)
            for w in (1, 0):
                last_copy(dr, w).start()
            gate_copy(dr, 2).wait_recv()
            gsend[dr, 0] = gate_sum() + grecv[dr, 1]
            gate_copy(dr, 1).start()

    def backward(jj, carry):
        d = 4 - jj
        right = lax.rem(z + d, NZ)
        chunk(right, logit_b, d - 1, lg_a, igp_a, lax.rem(z + NZ - d, NZ), lg_b, igp_b)
        send(0, jj)
        chunk(lax.rem(z + NZ - (d - 1), NZ), logit_a, d - 1, lg_b, igp_b, right, lg_a, igp_a)

        @pl.when(jj == 0)
        def _():
            for h in range(2):
                sbuf[h, 3, h] = item_sum(h).astype(BF16)
                rs_copy(h, 4, h).start()
            gsend[0, 3] = gate_sum()
            gate_copy(0, 4).start()

        send(1, jj)
        return carry

    lax.fori_loop(0, NZ // 2, backward, 0)

    for k in range(K):
        ugsend[k : k + 1, :] = jnp.sum(ugv[k], axis=0, keepdims=True)
    ug_sends = [rc(ugsend, ugrecv.at[i], ugs_s.at[i], ugs_r.at[i], quad[i]) for i in range(3)]
    for s in ug_sends:
        s.start()

    def u_core(hh, p):
        h = 1 - x if hh == 0 else x
        at = pl.ds(pl.multiple_of(h * UB + p * CH, CH), CH)
        return rc(uacc.at[1 - c, at, :], urecv.at[hh, p], uc_s.at[hh, p], uc_r.at[hh, p], cp)

    def u_x(p):
        return rc(usend.at[p], uxrecv.at[p], ux_s.at[p], ux_r.at[p], xp)

    def core_sum(hh, p):
        h = 1 - x if hh == 0 else x
        at = pl.ds(pl.multiple_of(h * UB + p * CH, CH), CH)
        u_core(hh, p).wait_recv()
        return uacc[c, at, :] + urecv[hh, p]

    for hh in range(2):
        for p in range(2):
            h = 1 - x if hh == 0 else x
            matmuls(z, lg_b, igp_b, 2 * h + p)
            u_core(hh, p).start()
    for p in range(2):
        usend[p] = core_sum(0, p).astype(BF16)
        u_x(p).start()

    sums = [item_sum(h) for h in range(2)]
    first = jnp.broadcast_to(x, (CH, UB)) == 0
    isend[...] = jnp.where(first, sums[1], sums[0]).astype(BF16)
    keep = jnp.where(first, sums[0], sums[1])
    i_x = rc(isend, irecv, fx_s.at[0], fx_r.at[0], xp)
    i_x.start()
    gate = gate_sum()
    for dr in range(2):
        gate_copy(dr, 1).wait_recv()
        gate = gate + grecv[dr, 0]
    igx[0] = gate
    ig_x = rc(igx.at[0], igx.at[1], fx_s.at[1], fx_r.at[1], xp)
    ig_x.start()

    for p in range(2):
        ukeep[p * CH : (p + 1) * CH, :] = core_sum(1, p)
    for s in ug_sends:
        s.wait_recv()
    ugate = (ugsend[...] + ugrecv[0]) + (ugrecv[1] + ugrecv[2])
    ugate = jnp.where(jnp.broadcast_to(c, (K, UB)) == 0, ugate[:, :UB], ugate[:, UB:])
    ugate_ref[...] = jnp.where(jnp.broadcast_to(x, (4, UB)) == 0, ugate[:4], ugate[4:])

    for dr in range(2):
        last_copy(dr, 0).wait_recv()
    ig_ref[own_rows, :] = keep + (rbuf[0, 0, 0].astype(F32) + rbuf[1, 0, 0].astype(F32))
    for dr in range(2):
        last_copy(dr, 1).wait_recv()
    i_x.wait_recv()
    ig_ref[peer_rows, :] = irecv[...].astype(F32) + (
        rbuf[0, 0, 1].astype(F32) + rbuf[1, 0, 1].astype(F32)
    )
    ig_x.wait_recv()
    mine, theirs = igx[0], igx[1]
    upper = jnp.concatenate([mine, theirs], axis=1)[:4]
    lower = jnp.concatenate([theirs, mine], axis=1)[4:]
    igate_ref[...] = jnp.where(jnp.broadcast_to(x, (4, UB)) == 0, upper, lower)
    for p in range(2):
        u_x(p).wait_recv()
        at = slice(p * CH, (p + 1) * CH)
        ug_ref[:, at] = (ukeep[at, :] + uxrecv[p].astype(F32)).T

    for s in (x_item, q_x, q_c, q_f, *u_sends, *st_sends, i_x, ig_x, *ug_sends):
        s.wait_send()
    for p in range(2):
        u_x(p).wait_send()
        for hh in range(2):
            u_core(hh, p).wait_send()
    gate_copy(0, 4).wait_send()
    for dr in range(2):
        rs_copy(dr, 4, dr).wait_send()
        for d in (1, 2, 3):
            gate_copy(dr, d).wait_send()
        for w in range(2):
            last_copy(dr, w).wait_send()
            for d in (2, 3):
                rs_copy(dr, d, w).wait_send()
        for hh in range(2):
            for s in range(1, 5 if hh == dr else 4):
                for n in range(2):
                    hop(dr, s, hh, n).wait_send()


def write_out(loss, ug, ig, ugate, igate, *outs):
    for a, o in zip((loss, ug, ig, ugate, igate), outs):
        o[...] = a[...]


def body(query, candidate, query_gate, candidate_gate, slope, scale, target):
    vmem = pl.BlockSpec(memory_space=pltpu.VMEM)
    smem = pl.BlockSpec(memory_space=pltpu.SMEM)
    dma = pltpu.SemaphoreType.DMA
    scratch = [
        pltpu.VMEM((2, 2, UB, UB), BF16),
        pltpu.VMEM((4, 8, UB), F32),
        pltpu.VMEM((NZ, 2, SLOT, UB), BF16),
        pltpu.VMEM((SLOT, UB), BF16),
        pltpu.VMEM((CH, CH), F32),
        pltpu.VMEM((CH, CH), F32),
        pltpu.VMEM((CH, CH), F32),
        pltpu.VMEM((CH, CH), F32),
        pltpu.VMEM((NZ, K * 64, CH), BF16),
        pltpu.VMEM((K, US, CH), BF16),
        pltpu.VMEM((K, 8, US), F32),
        pltpu.VMEM((8, US), F32),
        pltpu.VMEM((NZ // 2, K, CH, US), F32),
        pltpu.VMEM((NZ // 2, K, CH, US), F32),
        pltpu.VMEM((NZ, K, CH, US), F32),
        pltpu.VMEM((NZ, CH, US), F32),
        pltpu.VMEM((NZ, CH, US), F32),
        pltpu.VMEM((8, US), F32),
        pltpu.VMEM((8, US), F32),
        pltpu.VMEM((8, US), F32),
        pltpu.VMEM((4, 8, US), F32),
        pltpu.VMEM((8, US), F32),
        pltpu.VMEM((K * CH, US), BF16),
        pltpu.VMEM((K * CH, US), BF16),
        pltpu.VMEM((4, CH, 2 * CH), F32),
        pltpu.VMEM((4, CH, 2 * CH), F32),
        pltpu.VMEM((4, 8, CH), F32),
        pltpu.VMEM((K, 8, US), F32),
        pltpu.VMEM((2, US, UB), F32),
        pltpu.VMEM((4, CH, CH), F32),
        pltpu.VMEM((4, US, CH), BF16),
        pltpu.VMEM((2, 4, 2, CH, UB), BF16),
        pltpu.VMEM((2, 4, 2, CH, UB), BF16),
        pltpu.VMEM((2, 4, K, CH), F32),
        pltpu.VMEM((2, 4, K, CH), F32),
        pltpu.VMEM((2, 2, CH, UB), F32),
        pltpu.VMEM((UB, UB), F32),
        pltpu.VMEM((2, CH, UB), BF16),
        pltpu.VMEM((2, CH, UB), BF16),
        pltpu.VMEM((CH, UB), BF16),
        pltpu.VMEM((CH, UB), BF16),
        pltpu.VMEM((2, K, CH), F32),
        pltpu.VMEM((K, US), F32),
        pltpu.VMEM((3, K, US), F32),
        dma((1,)), dma((1,)),
        dma((3,)), dma((3,)),
        dma((3,)), dma((3,)),
        dma((2, 4, 2, 2)), dma((2, 4, 2, 2)),
        dma((3,)), dma((3,)),
        dma((2, 4, 2)), dma((2, 4, 2)),
        dma((2, 4)), dma((2, 4)),
        dma((2, 2)), dma((2, 2)),
        dma((2,)), dma((2,)),
        dma((2,)), dma((2,)),
        dma((3,)), dma((3,)),
    ]
    outs = (
        jax.ShapeDtypeStruct((1, UB), F32),
        jax.ShapeDtypeStruct((UB, UB), F32),
        jax.ShapeDtypeStruct((UB, UB), F32),
        jax.ShapeDtypeStruct((4, UB), F32),
        jax.ShapeDtypeStruct((4, UB), F32),
    )
    results = pl.pallas_call(
        kernel,
        out_shape=outs,
        in_specs=[vmem, vmem, vmem, vmem, smem, smem, vmem],
        out_specs=(vmem,) * 5,
        scratch_shapes=scratch,
        compiler_params=pltpu.CompilerParams(
            collective_id=0, has_side_effects=True, vmem_limit_bytes=60 * 1024 * 1024
        ),
    )(query, candidate, query_gate, candidate_gate, slope, scale, target.reshape(1, UB))
    loss, ug, ig, ugate, igate = pl.pallas_call(
        write_out, out_shape=outs, in_specs=[vmem] * 5, out_specs=(vmem,) * 5
    )(*results)
    return loss.reshape(UB), ug, ig, ugate, igate


def solution(mesh):
    in_specs = (
        P(("task", "blk"), "comp"),
        P(("task", "blk"), "comp"),
        P("comp", ("task", "blk")),
        P("comp", ("task", "blk")),
        P(),
        P("task"),
        P(("task", "blk")),
    )
    out_specs = (
        P(("task", "blk")),
        P(("task", "blk"), "comp"),
        P(("task", "blk"), "comp"),
        P("comp", ("task", "blk")),
        P("comp", ("task", "blk")),
    )
    return jax.shard_map(body, mesh=mesh, in_specs=in_specs, out_specs=out_specs, check_vma=False)
```
